32 devices in a mesh: groups: 2 (over x), row: 4 (over y, core), col: 4 (over z).
Axes of the slice: x: 2, y: 2, z: 4, core: 2. Of those that a mesh axis runs over, the one named last changes fastest.
Arguments:
- hamiltonian: bfloat16 [256, 64, 1536], P(('groups', 'row'), None, 'col'), parts along dimension 0, may hold values from -0.15625 to 0.15625
- columns: int32 [256, 24], P(('groups', 'row'), 'col'), parts along dimension 0, may hold values from 0 to 31
- vectors: bfloat16 [16384, 192], P(('groups', 'row', 'col')), parts along dimension 0, may hold values from -40 to 40
- lower: float32 [2], P('groups'), parts along dimension 0, may hold values from -2.4 to -1.6
- upper: float32 [2], P('groups'), parts along dimension 0, may hold values from 0.8 to 1.6
Outputs:
- basis: float32 [16384, 192], P(('groups', 'row', 'col')), parts along dimension 0
The draws below stay inside these ranges and needn't reach their ends.
There are 2 independent parts, one for each index of `groups`. The reference program is written for one: setup_inputs(seed, part) draws one part's arguments, and reference() takes and returns one part's arrays. A program takes and returns all parts, laid end to end along the dimension named above; each array names one. Nothing has to cross between parts.
Inputs may be any that keep to these rules, and one draw needn't show every extreme that they name: Index of a block column among the 32 block columns of the slot's column group.
All inputs are finite; a program needn't handle non-finite values.
Results may differ from the reference program's by a relative error of at most 0.015.
Values may be sent and summed in bfloat16 or wider, within the bound.
No kernel may reach another device: no remote copies, remote signals or barrier semaphores. Data moves between devices by JAX's collectives and lax.ppermute only.
A program may use at most 64 MiB of HBM per device.

```python
import math
import jax
import jax.numpy as jnp
from jax import lax

BS = 64
NV = 192
KL = 6
BD = 8
NB = 128
ROWS = 8192
K = 24
PANEL = 32
N_COL = 4


def draw_vectors(key, part):
    key = jax.random.fold_in(key, 11)
    keys = jax.random.split(key, 4)
    noise = jax.random.normal(keys[0], (ROWS, NV), jnp.float32)
    jitter = jnp.exp(jax.random.uniform(keys[1], (ROWS, 1), jnp.float32, 0.0, math.log(3.0)))
    weight = 0.8
    row_common = jax.random.normal(keys[2], (ROWS, 1), jnp.float32)
    col_loads = jax.random.uniform(keys[3], (1, NV), jnp.float32, -1.0, 1.0)
    position = jnp.arange(ROWS, dtype=jnp.float32) / ROWS
    rising = jnp.exp(position * math.log(4.0))[:, None]
    values = (noise + weight * row_common * col_loads) * rising * jitter * 0.5
    return jnp.clip(values, -40.0, 40.0).astype(jnp.bfloat16)


def touch_ends(values, own_key, smallest, largest):
    longest = values.shape.index(max(values.shape))
    spots = []
    for shift in (0, 1):
        where = [jax.random.randint(jax.random.fold_in(own_key, axis), (), 0, length) for axis, length in enumerate(values.shape)]
        where[longest] = (where[longest] + shift) % values.shape[longest]
        spots.append(tuple(where))
    return values.at[spots[0]].set(smallest).at[spots[1]].set(largest)


def shard_levels(stream_key, shape, cuts, low, top_value):
    def one(axis_at, parts):
        draws = jax.random.uniform(jax.random.fold_in(jax.random.fold_in(stream_key, 6), axis_at), (parts,), jnp.float32, low / len(cuts), top_value / len(cuts))
        return jnp.repeat(jnp.exp(draws), shape[axis_at] // parts).reshape((-1,) + (1,) * (len(shape) - axis_at - 1))

    loudness = one(*cuts[0])
    for cut in cuts[1:]:
        loudness = loudness * one(*cut)
    return loudness


def normal_values(rng, dims, scale, most, pieces=(), held_as=jnp.bfloat16):
    result = jax.random.normal(rng, dims, jnp.float32) * scale
    if len(pieces) > 0:
        result = shard_levels(rng, dims, pieces, -0.22, 0.18) * result
    return jnp.clip(result, min=-most, max=most).astype(held_as)


def setup_inputs(seed: int = 0, part: int = 0) -> dict:
    key_of = jax.random.split(jax.random.key(seed), 6)
    part_splits = jax.random.split(jax.random.fold_in(key_of[5], part), 6)
    hamiltonian = normal_values(part_splits[0], (NB, BS, K * BS), (K * BS) ** -0.5, 0.15625, ((0, 4), (2, 4)))
    columns = touch_ends(jax.random.randint(part_splits[1], (NB, K), 0, PANEL), jax.random.fold_in(part_splits[1], 1), 0, PANEL - 1).astype(jnp.int32)
    vectors = draw_vectors(jax.random.fold_in(jax.random.fold_in(key_of[5], part), 71), part)
    lower = jnp.clip(jax.random.uniform(part_splits[3], (1,), jnp.float32, -2.4, -1.6), -2.4, -1.6)
    upper = jnp.clip(jax.random.uniform(part_splits[4], (1,), jnp.float32, 0.8, 1.6), 0.8, 1.6)
    return dict(hamiltonian=hamiltonian, columns=columns, vectors=vectors, lower=lower, upper=upper)


def apply_matrix(hamiltonian, columns, source):
    blocks = source.reshape(NB, BS, NV).astype(jnp.float32)
    summed = jnp.zeros((NB, BS, NV), jnp.float32)
    for group in range(N_COL):
        local_ids = columns[:, group * KL:(group + 1) * KL]
        global_ids = (local_ids // BD * N_COL + group) * BD + local_ids % BD
        picked = jnp.take(blocks, global_ids.astype(jnp.int32), axis=0).reshape(NB, KL * BS, NV)
        part_h = hamiltonian[:, :, group * KL * BS:(group + 1) * KL * BS].astype(jnp.float32)
        partial_value = jnp.einsum('rik,rkn->rin', part_h, picked)
        rounded = lax.optimization_barrier(partial_value.astype(jnp.bfloat16))
        summed = summed + rounded.astype(jnp.float32)
    return summed.reshape(ROWS, NV)

def reference(hamiltonian, columns, vectors, lower, upper):
    center = (upper[0] + lower[0]) * 0.5
    spread = (upper[0] - lower[0]) * 0.5
    start_vec = vectors.astype(jnp.float32)
    product = apply_matrix(hamiltonian, columns, vectors)
    first_filter = ((product - center * start_vec) / spread).astype(jnp.bfloat16)
    product = apply_matrix(hamiltonian, columns, first_filter)
    second_filter = (2.0 * (product - center * first_filter.astype(jnp.float32)) / spread - start_vec).astype(jnp.bfloat16)
    gram = jnp.dot(second_filter.T.astype(jnp.float32), second_filter.astype(jnp.float32), preferred_element_type=jnp.float32) / ROWS
    lower_factor = jnp.linalg.cholesky(gram)
    basis = lax.linalg.triangular_solve(lower_factor, second_filter.astype(jnp.float32), left_side=False, lower=True, transpose_a=True)
    return basis
```

```python
import functools

import jax
import jax.numpy as jnp
from jax import lax
from jax.experimental import pallas as pl
from jax.experimental.pallas import tpu as pltpu
from jax.sharding import PartitionSpec as P

LANES = 128
F32 = jnp.float32
BF16 = jnp.bfloat16
VMEM = pl.BlockSpec(memory_space=pltpu.VMEM)
SMEM = pl.BlockSpec(memory_space=pltpu.SMEM)


def call(kernel, out_shape, in_specs, scratch=(), flops=1000, name=None):
    return pl.pallas_call(
        kernel,
        out_shape=out_shape,
        in_specs=in_specs,
        out_specs=jax.tree.map(lambda _: VMEM, out_shape),
        scratch_shapes=list(scratch),
        compiler_params=pltpu.CompilerParams(vmem_limit_bytes=40 * 1024 * 1024),
        cost_estimate=pl.CostEstimate(flops=flops, bytes_accessed=1000, transcendentals=0),
        name=name,
    )


def swap(x, axis, key):
    count = lax.axis_size(axis)
    return lax.ppermute(x, axis, [(i, i ^ key) for i in range(count)])


def gather_shards(own):
    shards = {0: own}
    bit = lax.axis_size("row") // 2
    while bit:
        for key in list(shards):
            shards[key | bit] = swap(shards[key], "row", bit)
        bit //= 2
    return [shards[key] for key in range(len(shards))]


def pack(vectors):
    half = vectors.shape[0] // 2
    return vectors[:, :LANES], jnp.concatenate(
        [vectors[:half, LANES:], vectors[half:, LANES:]], axis=1
    )


def product_kernel(n_row, n_col, orbitals, place_ref, ids_ref, ham_ref, *refs):
    wide, thin = refs[:n_row], refs[n_row : 2 * n_row]
    wide_out = refs[2 * n_row : 2 * n_row + n_col]
    thin_out = refs[2 * n_row + n_col : 2 * n_row + 2 * n_col]
    all_wide, left, right = refs[2 * n_row + 2 * n_col :]
    rows = wide[0].shape[0]
    half = rows // 2
    own_blocks = rows // orbitals
    slots = ids_ref.shape[1]
    row_at, col_at = place_ref[0], place_ref[1]
    low_lane = lax.broadcasted_iota(jnp.int32, (half, LANES), 1) < LANES // 2
    zero = jnp.zeros((half, LANES), BF16)
    for key in range(n_row):
        base = key * rows
        all_wide[pl.ds(base, rows), :] = wide[key][...]
        packed = thin[key][...]
        turned = jnp.concatenate([packed[:, LANES // 2 :], packed[:, : LANES // 2]], axis=1)
        left[pl.ds(base, half), :] = jnp.where(low_lane, packed, zero)
        right[pl.ds(base, half), :] = jnp.where(low_lane, zero, turned)
        left[pl.ds(base + half, half), :] = jnp.where(low_lane, turned, zero)
        right[pl.ds(base + half, half), :] = jnp.where(low_lane, zero, packed)

    def starts(block_row):
        out = []
        for slot in range(slots):
            index = ids_ref[block_row, slot]
            owner = lax.div(index, own_blocks)
            inner = index - owner * own_blocks
            out.append(pl.multiple_of(((owner ^ row_at) * own_blocks + inner) * orbitals, orbitals))
        return out

    def picked(ref, where):
        return jnp.concatenate([ref[pl.ds(at, orbitals), :] for at in where], axis=0)

    for key in range(n_col):
        first = (key ^ col_at) * own_blocks

        def body(step, carry, key=key, first=first):
            upper, lower = step, step + own_blocks // 2
            up_at, low_at = starts(first + upper), starts(first + lower)
            up_ham, low_ham = ham_ref[first + upper], ham_ref[first + lower]
            dot = functools.partial(jnp.dot, preferred_element_type=F32)
            up_rows = pl.ds(pl.multiple_of(upper * orbitals, orbitals), orbitals)
            low_rows = pl.ds(pl.multiple_of(lower * orbitals, orbitals), orbitals)
            wide_out[key][up_rows, :] = dot(up_ham, picked(all_wide, up_at)).astype(BF16)
            wide_out[key][low_rows, :] = dot(low_ham, picked(all_wide, low_at)).astype(BF16)
            thin_out[key][up_rows, :] = (
                dot(up_ham, picked(left, up_at)) + dot(low_ham, picked(right, low_at))
            ).astype(BF16)
            return carry

        lax.fori_loop(0, own_blocks // 2, body, 0, unroll=True)


def product(place, ids, ham, wide, thin):
    n_row, n_col = len(wide), lax.axis_size("col")
    rows = wide[0].shape[0]
    total = rows * n_row
    wide_shape = jax.ShapeDtypeStruct((rows, LANES), BF16)
    thin_shape = jax.ShapeDtypeStruct((rows // 2, LANES), BF16)
    outs = call(
        functools.partial(product_kernel, n_row, n_col, ham.shape[1]),
        [wide_shape] * n_col + [thin_shape] * n_col,
        [SMEM, SMEM, VMEM] + [VMEM] * (2 * n_row),
        [pltpu.VMEM((total, LANES), BF16)] * 3,
        flops=2 * ham.shape[0] * ham.shape[1] * ham.shape[2] * 256,
        name="product",
    )(place, ids, ham, *wide, *thin)
    return outs[:n_col], outs[n_col:]


def exchange(terms):
    got = {0: terms[0]}
    for key in reversed(range(1, len(terms))):
        got[key] = swap(terms[key], "col", key)
    return [got[key] for key in range(len(terms))]


def ends(lower_ref, upper_ref, shape):
    low = jnp.full(shape, lower_ref[0], F32)
    high = jnp.full(shape, upper_ref[0], F32)
    return (high + low) * 0.5, 1.0 / ((high - low) * 0.5)


def total_of(refs):
    acc = refs[0][...].astype(F32)
    for ref in refs[1:]:
        acc = acc + ref[...].astype(F32)
    return acc


def first_kernel(n_col, lower_ref, upper_ref, wide_v, thin_v, *refs):
    center, scale = ends(lower_ref, upper_ref, (1, LANES))
    parts = ((wide_v, refs[:n_col], refs[2 * n_col]), (thin_v, refs[n_col : 2 * n_col], refs[-1]))
    for start, terms, out in parts:
        out[...] = ((total_of(terms) - center * start[...].astype(F32)) * scale).astype(BF16)


def second_kernel(n_col, rows_all, place_ref, lower_ref, upper_ref, wide_v, thin_v, wide_f, thin_f, *refs):
    wide_terms, thin_terms = refs[:n_col], refs[n_col : 2 * n_col]
    wide_out, thin_out, keep_out, send_out, gram = refs[2 * n_col :]
    center, scale = ends(lower_ref, upper_ref, (1, LANES))
    parts = ((wide_v, wide_f, wide_terms, wide_out), (thin_v, thin_f, thin_terms, thin_out))
    for start, first, terms, out in parts:
        moved = total_of(terms) - center * first[...].astype(F32)
        out[...] = (2.0 * moved * scale - start[...].astype(F32)).astype(BF16)
    wide, thin = wide_out[...], thin_out[...]
    half = thin.shape[0]
    size = LANES // 2

    def cross(a, b):
        return lax.dot_general(a, b, (((0,), (0,)), ((), ())), preferred_element_type=F32)

    inv = 1.0 / rows_all
    aa = cross(wide, wide) * inv
    upper = cross(thin, wide[:half]) * inv
    lower = cross(thin, wide[half:]) * inv
    bb = cross(thin, thin) * inv
    turned = jnp.concatenate([bb[:size, size:], bb[:size, :size]], axis=1)
    low_lane = lax.broadcasted_iota(jnp.int32, (size, LANES), 1) < size
    gram[pl.ds(0, size), :] = jnp.where(low_lane, aa[:size], turned + bb[size:])
    gram[pl.ds(size, size), :] = aa[size:]
    gram[pl.ds(2 * size, size), :] = upper[:size] + lower[size:]
    part = 3 * size // 2
    mine = place_ref[0] & 1
    keep_out[...] = gram[pl.ds(pl.multiple_of(mine * part, 8), part), :]
    send_out[...] = gram[pl.ds(pl.multiple_of((1 - mine) * part, 8), part), :]


def inverse_factor(block, pivots):
    size = block.shape[0]
    tiles = size // 8
    rows = lax.broadcasted_iota(jnp.int32, (8, LANES), 0)
    lanes = lax.broadcasted_iota(jnp.int32, (8, LANES), 1)
    pad = jnp.concatenate([block, jnp.zeros((size, LANES - size), F32)], axis=1)
    a = [
        jnp.where(lanes == rows + (size + 8 * t), 1.0, pad[8 * t : 8 * t + 8]) for t in range(tiles)
    ]
    diag = [jnp.ones((8, LANES), F32) for _ in range(tiles)]
    full = (8, LANES)
    for j in range(0, size, pivots):
        t0, s0 = divmod(j, 8)
        cols = [
            [jnp.broadcast_to(a[t][:, j + k : j + k + 1], full) for t in range(t0, tiles)]
            for k in range(pivots)
        ]
        lines = [jnp.broadcast_to(a[t0][s0 + k : s0 + k + 1, :], full) for k in range(pivots)]
        small = [
            [jnp.broadcast_to(cols[q][0][s0 + k : s0 + k + 1, :], full) for q in range(k + 1)]
            for k in range(pivots)
        ]
        for k in range(pivots):
            d = small[k][k]
            diag[t0] = jnp.where(rows == s0 + k, d, diag[t0])
            r = 1.0 / d
            mult = {}
            for q in range(k + 1, pivots):
                mult[q] = small[q][k] * r
            for q in range(k + 1, pivots):
                lines[q] = lines[q] - mult[q] * lines[k]
                for p in range(k + 1, q + 1):
                    small[q][p] = small[q][p] - mult[q] * small[p][k]
            for i, t in enumerate(range(t0, tiles)):
                x = cols[k][i] * r
                if t == t0:
                    x = jnp.where(rows > s0 + k, x, 0.0)
                for q in range(k + 1, pivots):
                    cols[q][i] = cols[q][i] - cols[k][i] * mult[q]
                a[t] = a[t] - x * lines[k]
    out = jnp.concatenate([a[t] * lax.rsqrt(diag[t]) for t in range(tiles)], axis=0)
    return out[:, size:]


def last_kernel(pivots, place_ref, keep_ref, other_ref, wide_ref, thin_ref, out_ref, gram, factor):
    size = LANES // 2
    part = 3 * size // 2
    mine = place_ref[0] & 1
    gram[pl.ds(pl.multiple_of(mine * part, 8), part), :] = keep_ref[...]
    gram[pl.ds(pl.multiple_of((1 - mine) * part, 8), part), :] = other_ref[...]
    dot = functools.partial(
        jnp.dot, precision=lax.Precision.HIGHEST, preferred_element_type=F32
    )

    def dot_t(a, b):
        return lax.dot_general(
            a,
            b,
            (((1,), (1,)), ((), ())),
            precision=lax.Precision.HIGHEST,
            preferred_element_type=F32,
        )

    g00 = gram[pl.ds(0, size), :][:, :size]
    g22 = gram[pl.ds(0, size), :][:, size:]
    strip = gram[pl.ds(size, 2 * size), :]
    x0 = inverse_factor(g00, pivots)
    l_strip = dot_t(strip[:, :size], x0)
    rest = strip[:, size:] - dot_t(l_strip, l_strip[:size])
    x1 = inverse_factor(rest[:size], pivots)
    l10, l20 = l_strip[:size], l_strip[size:]
    l21 = dot_t(rest[size:], x1)
    x2 = inverse_factor(g22 - dot_t(l20, l20) - dot_t(l21, l21), pivots)
    n10 = -dot(x1, dot(l10, x0))
    n20 = -dot(x2, dot(l20, x0) + dot(l21, n10))
    n21 = -dot(x2, dot(l21, x1))
    zero = jnp.zeros((size, size), F32)
    factor[pl.ds(0, size), :] = jnp.concatenate([x0, zero], axis=1)
    factor[pl.ds(size, size), :] = jnp.concatenate([n10, x1], axis=1)
    factor[pl.ds(2 * size, size), :] = jnp.concatenate([n20, n21], axis=1)

    def apply(mat, vec):
        high = mat.astype(BF16)
        low = (mat - high.astype(F32)).astype(BF16)
        con = (((1,), (1,)), ((), ()))
        return lax.dot_general(high, vec, con, preferred_element_type=F32) + lax.dot_general(
            low, vec, con, preferred_element_type=F32
        )

    wide, thin = wide_ref[...], thin_ref[...]
    half = thin.shape[0]
    main = apply(factor[...], wide)
    out_ref[pl.ds(0, 2 * size), :] = main[: 2 * size]
    tail = jnp.concatenate(
        [
            apply(jnp.concatenate([x2, zero], axis=1), thin),
            apply(jnp.concatenate([zero, x2], axis=1), thin),
        ],
        axis=1,
    )
    out_ref[pl.ds(2 * size, size), :] = main[2 * size :] + tail


def sum_all(keep, send):
    acc = keep + swap(send, "row", 1)
    bit = 2
    while bit < lax.axis_size("row"):
        acc = acc + swap(acc, "row", bit)
        bit *= 2
    got = [swap(acc, "col", key) for key in range(1, lax.axis_size("col"))]
    for x in got:
        acc = acc + x
    return acc, swap(acc, "row", 1)


def per_device(hamiltonian, columns, vectors, lower, upper):
    rows = vectors.shape[0]
    n_col = lax.axis_size("col")
    place = jnp.stack([lax.axis_index("row"), lax.axis_index("col")]).astype(jnp.int32)
    wide_shape = jax.ShapeDtypeStruct((rows, LANES), BF16)
    thin_shape = jax.ShapeDtypeStruct((rows // 2, LANES), BF16)
    half_gram = jax.ShapeDtypeStruct((96, LANES), F32)

    def apply(wide, thin):
        terms = product(place, columns, hamiltonian, gather_shards(wide), gather_shards(thin))
        return [*exchange(terms[0]), *exchange(terms[1])]

    wide_v, thin_v = pack(vectors)
    terms = apply(wide_v, thin_v)
    wide_f, thin_f = call(
        functools.partial(first_kernel, n_col),
        [wide_shape, thin_shape],
        [SMEM, SMEM] + [VMEM] * (2 + 2 * n_col),
        name="first_filter",
    )(lower, upper, wide_v, thin_v, *terms)
    terms = apply(wide_f, thin_f)
    rows_all = rows * n_col * lax.axis_size("row")
    wide_s, thin_s, keep, send = call(
        functools.partial(second_kernel, n_col, rows_all),
        [wide_shape, thin_shape, half_gram, half_gram],
        [SMEM, SMEM, SMEM] + [VMEM] * (4 + 2 * n_col),
        [pltpu.VMEM((192, LANES), F32)],
        name="second_filter",
    )(place, lower, upper, wide_v, thin_v, wide_f, thin_f, *terms)
    keep, other = sum_all(keep, send)
    basis = call(
        functools.partial(last_kernel, 2),
        jax.ShapeDtypeStruct((192, rows), F32),
        [SMEM] + [VMEM] * 4,
        [pltpu.VMEM((192, LANES), F32), pltpu.VMEM((192, LANES), F32)],
        name="orthonormalize",
    )(place, keep, other, wide_s, thin_s)
    return basis.T


def solution(mesh):
    return jax.shard_map(
        per_device,
        mesh=mesh,
        in_specs=(
            P(("groups", "row"), None, "col"),
            P(("groups", "row"), "col"),
            P(("groups", "row", "col"), None),
            P("groups"),
            P("groups"),
        ),
        out_specs=P(("groups", "row", "col"), None),
        check_vma=False,
    )
```

```python
import functools

import jax
import jax.numpy as jnp
from jax import lax
from jax.experimental import pallas as pl
from jax.experimental.pallas import tpu as pltpu
from jax.sharding import PartitionSpec as P

LANES = 128
SIZE = LANES // 2
PIVOTS = 8
F32 = jnp.float32
BF16 = jnp.bfloat16
VMEM = pl.BlockSpec(memory_space=pltpu.VMEM)
SMEM = pl.BlockSpec(memory_space=pltpu.SMEM)


def call(kernel, out_shape, in_specs, scratch=(), flops=1000, name=None):
    return pl.pallas_call(
        kernel,
        out_shape=out_shape,
        in_specs=in_specs,
        out_specs=jax.tree.map(lambda _: VMEM, out_shape),
        scratch_shapes=list(scratch),
        compiler_params=pltpu.CompilerParams(vmem_limit_bytes=40 * 1024 * 1024),
        cost_estimate=pl.CostEstimate(flops=flops, bytes_accessed=1000, transcendentals=0),
        name=name,
    )


def swap(x, axis, key):
    count = lax.axis_size(axis)
    return lax.ppermute(x, axis, [(i, i ^ key) for i in range(count)])


def gather_shards(own, twin):
    shards = {0: own}
    bit = lax.axis_size("row") // 2
    while bit:
        for key in list(shards):
            late = key == 0 and bit == 1
            shards[key | bit] = swap(twin if late else shards[key], "row", bit)
        bit //= 2
    return [shards[key] for key in range(len(shards))]


def pack_kernel(turned_ref, out):
    rows = turned_ref.shape[1]
    half = rows // 2
    turned = turned_ref[...].astype(F32)
    out[pl.ds(0, rows), :] = turned[:LANES].T.astype(BF16)
    thin = jnp.concatenate([turned[LANES:, :half], turned[LANES:, half:]], axis=0)
    out[pl.ds(rows, half), :] = thin.T.astype(BF16)


def load_kernel(own_blocks, orbitals, vec_ref, ids_ref, ham_ref, out, at_out):
    out[...] = vec_ref[...]
    at_out[...] = (ids_ref[...] ^ (lax.axis_index("row") * own_blocks)) * orbitals


def product_kernel(keys, n_row, own_blocks, at_ref, ham_ref, *refs):
    parts, outs = refs[:n_row], refs[n_row : n_row + len(keys)]
    source = refs[-1]
    orbitals = ham_ref.shape[1]
    rows = own_blocks * orbitals
    half = rows // 2
    me = lax.axis_index("col")
    first = [(key ^ me) * own_blocks for key in keys]
    low_lane = lax.broadcasted_iota(jnp.int32, (orbitals, LANES), 1) < SIZE
    for key in range(n_row):
        base = key * rows
        source[pl.ds(base, rows), pl.ds(0, LANES)] = parts[key][pl.ds(0, rows), :]
        thin = parts[key][pl.ds(rows, half), :]
        source[pl.ds(base, half), pl.ds(LANES, LANES)] = thin
        source[pl.ds(base + half, half), pl.ds(LANES, LANES)] = jnp.concatenate(
            [thin[:, SIZE:], thin[:, :SIZE]], axis=1
        )

    def term(i, block):
        picked = [
            source[pl.ds(pl.multiple_of(at_ref[slot, first[i] + block], orbitals), orbitals), :]
            for slot in range(at_ref.shape[0])
        ]
        return jnp.dot(
            ham_ref[first[i] + block],
            jnp.concatenate(picked, axis=0),
            preferred_element_type=F32,
        )

    for i, out in enumerate(outs):
        for block in range(own_blocks // 2):
            upper, lower = term(i, block), term(i, block + own_blocks // 2)
            out[pl.ds(block * orbitals, orbitals), :] = upper[:, :LANES].astype(BF16)
            out[pl.ds(half + block * orbitals, orbitals), :] = lower[:, :LANES].astype(BF16)
            turned = jnp.concatenate([lower[:, LANES + SIZE :], lower[:, LANES : LANES + SIZE]], axis=1)
            out[pl.ds(rows + block * orbitals, orbitals), :] = jnp.where(
                low_lane, upper[:, LANES:], turned
            ).astype(BF16)


def product(keys, own_blocks, at, ham, parts):
    n_row = len(parts)
    orbitals = ham.shape[1]
    flops = 4 * own_blocks * len(keys) * orbitals * ham.shape[2] * LANES
    return call(
        functools.partial(product_kernel, keys, n_row, own_blocks),
        [jax.ShapeDtypeStruct(parts[0].shape, BF16)] * len(keys),
        [SMEM, VMEM] + [VMEM] * n_row,
        [pltpu.VMEM((own_blocks * n_row * orbitals, 2 * LANES), BF16)],
        flops=flops,
        name="product",
    )(at, ham, *parts)


def add_kernel(a, b, later, out, later_out):
    out[...] = (a[...].astype(F32) + b[...].astype(F32)).astype(BF16)
    later_out[...] = later[...]


def add(a, b, later):
    shape = jax.ShapeDtypeStruct(a.shape, BF16)
    return call(add_kernel, [shape, shape], [VMEM] * 3, name="add")(a, b, later)


def summands(own_blocks, at, ham, parts):
    n_col = lax.axis_size("col")
    if n_col != 4:
        terms = product(tuple(range(n_col)), own_blocks, at, ham, parts)
        return [terms[0]] + [swap(terms[key], "col", key) for key in range(1, n_col)]
    (far,) = product((3,), own_blocks, at, ham, parts)
    other = swap(far, "col", 1)
    across, near, own = product((2, 1, 0), own_blocks, at, ham, parts)
    across, near = add(across, other, near)
    near = swap(near, "col", 1)
    return [own, swap(across, "col", 2), near]


def ends(lower_ref, upper_ref, shape):
    low = jnp.full(shape, lower_ref[0], F32)
    high = jnp.full(shape, upper_ref[0], F32)
    return (high + low) * 0.5, 1.0 / ((high - low) * 0.5)


def total_of(refs):
    acc = refs[0][...].astype(F32)
    for ref in refs[1:]:
        acc = acc + ref[...].astype(F32)
    return acc


def first_kernel(lower_ref, upper_ref, start, *refs):
    center, scale = ends(lower_ref, upper_ref, (1, LANES))
    moved = total_of(refs[:-1]) - center * start[...].astype(F32)
    refs[-1][...] = (moved * scale).astype(BF16)


def cross(a, b):
    return lax.dot_general(a, b, (((0,), (0,)), ((), ())), preferred_element_type=F32)


def second_kernel(rows_all, lower_ref, upper_ref, start, first, *refs):
    out, keep_out, send_out, gram = refs[-4:]
    center, scale = ends(lower_ref, upper_ref, (1, LANES))
    moved = total_of(refs[:-4]) - center * first[...].astype(F32)
    filtered = (2.0 * moved * scale - start[...].astype(F32)).astype(BF16)
    out[...] = filtered
    rows = out.shape[0] * 2 // 3
    half = rows // 2
    wide, thin = filtered[:rows], filtered[rows:]
    inv = 1.0 / rows_all
    aa = cross(wide, wide) * inv
    upper = cross(thin, wide[:half]) * inv
    lower = cross(thin, wide[half:]) * inv
    bb = cross(thin, thin) * inv
    turned = jnp.concatenate([bb[:SIZE, SIZE:], bb[:SIZE, :SIZE]], axis=1)
    low_lane = lax.broadcasted_iota(jnp.int32, (SIZE, LANES), 1) < SIZE
    gram[pl.ds(0, SIZE), :] = jnp.where(low_lane, aa[:SIZE], turned + bb[SIZE:])
    gram[pl.ds(SIZE, SIZE), :] = aa[SIZE:]
    gram[pl.ds(2 * SIZE, SIZE), :] = upper[:SIZE] + lower[SIZE:]
    part = 3 * SIZE // 2
    mine = lax.axis_index("row") & 1
    keep_out[...] = gram[pl.ds(pl.multiple_of(mine * part, 8), part), :]
    send_out[...] = gram[pl.ds(pl.multiple_of((1 - mine) * part, 8), part), :]


def inverse_factor(block, pivots):
    size = block.shape[0]
    tiles = size // 8
    rows = lax.broadcasted_iota(jnp.int32, (8, LANES), 0)
    lanes = lax.broadcasted_iota(jnp.int32, (8, LANES), 1)
    pad = jnp.concatenate([block, jnp.zeros((size, LANES - size), F32)], axis=1)
    a = [
        jnp.where(lanes == rows + (size + 8 * t), 1.0, pad[8 * t : 8 * t + 8]) for t in range(tiles)
    ]
    diag = [jnp.ones((8, LANES), F32) for _ in range(tiles)]
    full = (8, LANES)
    for j in range(0, size, pivots):
        t0, s0 = divmod(j, 8)
        cols = [
            [jnp.broadcast_to(a[t][:, j + k : j + k + 1], full) for t in range(t0, tiles)]
            for k in range(pivots)
        ]
        lines = [jnp.broadcast_to(a[t0][s0 + k : s0 + k + 1, :], full) for k in range(pivots)]
        small = [
            [jnp.broadcast_to(cols[q][0][s0 + k : s0 + k + 1, :], full) for q in range(k + 1)]
            for k in range(pivots)
        ]
        for k in range(pivots):
            d = small[k][k]
            diag[t0] = jnp.where(rows == s0 + k, d, diag[t0])
            r = 1.0 / d
            mult = {}
            for q in range(k + 1, pivots):
                mult[q] = small[q][k] * r
            for q in range(k + 1, pivots):
                lines[q] = lines[q] - mult[q] * lines[k]
                for p in range(k + 1, q + 1):
                    small[q][p] = small[q][p] - mult[q] * small[p][k]
            for i, t in enumerate(range(t0, tiles)):
                x = cols[k][i] * r
                if t == t0:
                    x = jnp.where(rows > s0 + k, x, 0.0)
                for q in range(k + 1, pivots):
                    cols[q][i] = cols[q][i] - cols[k][i] * mult[q]
                a[t] = a[t] - x * lines[k]
    out = jnp.concatenate([a[t] * lax.rsqrt(diag[t]) for t in range(tiles)], axis=0)
    return out[:, size:]


def last_kernel(pivots, keep_ref, other_ref, vec_ref, out_ref, gram, factor):
    size = LANES // 2
    part = 3 * size // 2
    mine = lax.axis_index("row") & 1
    gram[pl.ds(pl.multiple_of(mine * part, 8), part), :] = keep_ref[...]
    gram[pl.ds(pl.multiple_of((1 - mine) * part, 8), part), :] = other_ref[...]
    dot = functools.partial(
        jnp.dot, precision=lax.Precision.HIGHEST, preferred_element_type=F32
    )

    def dot_t(a, b):
        return lax.dot_general(
            a,
            b,
            (((1,), (1,)), ((), ())),
            precision=lax.Precision.HIGHEST,
            preferred_element_type=F32,
        )

    g00 = gram[pl.ds(0, size), :][:, :size]
    g22 = gram[pl.ds(0, size), :][:, size:]
    strip = gram[pl.ds(size, 2 * size), :]
    x0 = inverse_factor(g00, pivots)
    l_strip = dot_t(strip[:, :size], x0)
    rest = strip[:, size:] - dot_t(l_strip, l_strip[:size])
    x1 = inverse_factor(rest[:size], pivots)
    l10, l20 = l_strip[:size], l_strip[size:]
    l21 = dot_t(rest[size:], x1)
    x2 = inverse_factor(g22 - dot_t(l20, l20) - dot_t(l21, l21), pivots)
    n10 = -dot(x1, dot(l10, x0))
    n20 = -dot(x2, dot(l20, x0) + dot(l21, n10))
    n21 = -dot(x2, dot(l21, x1))
    zero = jnp.zeros((size, size), F32)
    factor[pl.ds(0, size), :] = jnp.concatenate([x0, zero], axis=1)
    factor[pl.ds(size, size), :] = jnp.concatenate([n10, x1], axis=1)
    factor[pl.ds(2 * size, size), :] = jnp.concatenate([n20, n21], axis=1)

    def apply(mat, vec):
        high = mat.astype(BF16)
        low = (mat - high.astype(F32)).astype(BF16)
        con = (((1,), (1,)), ((), ()))
        return lax.dot_general(high, vec, con, preferred_element_type=F32) + lax.dot_general(
            low, vec, con, preferred_element_type=F32
        )

    rows = out_ref.shape[1]
    wide, thin = vec_ref[pl.ds(0, rows), :], vec_ref[pl.ds(rows, rows // 2), :]
    main = apply(factor[...], wide)
    out_ref[pl.ds(0, 2 * size), :] = main[: 2 * size]
    tail = jnp.concatenate(
        [
            apply(jnp.concatenate([x2, zero], axis=1), thin),
            apply(jnp.concatenate([zero, x2], axis=1), thin),
        ],
        axis=1,
    )
    out_ref[pl.ds(2 * size, size), :] = main[2 * size :] + tail


def sum_all(keep, send):
    acc = keep + swap(send, "row", 1)
    bit = 2
    while bit < lax.axis_size("row"):
        acc = acc + swap(acc, "row", bit)
        bit *= 2
    got = [swap(acc, "col", key) for key in range(1, lax.axis_size("col"))]
    for x in got:
        acc = acc + x
    return acc, swap(acc, "row", 1)


def per_device(hamiltonian, columns, vectors, lower, upper):
    rows = vectors.shape[0]
    orbitals = hamiltonian.shape[1]
    own_blocks = rows // orbitals
    rows_all = rows * lax.axis_size("col") * lax.axis_size("row")
    shape = jax.ShapeDtypeStruct((rows + rows // 2, LANES), BF16)
    half_gram = jax.ShapeDtypeStruct((3 * SIZE // 2, LANES), F32)
    gram = pltpu.VMEM((3 * SIZE, LANES), F32)

    start = call(pack_kernel, shape, [VMEM], name="pack")(vectors.T)
    twin, at = call(
        functools.partial(load_kernel, own_blocks, orbitals),
        [shape, jax.ShapeDtypeStruct(columns.shape[::-1], jnp.int32)],
        [VMEM, VMEM, VMEM],
        name="load",
    )(start, columns.T, hamiltonian)
    terms = summands(own_blocks, at, hamiltonian, gather_shards(start, twin))
    first = call(
        first_kernel, shape, [SMEM, SMEM] + [VMEM] * (1 + len(terms)), name="first_filter"
    )(lower, upper, start, *terms)
    terms = summands(own_blocks, at, hamiltonian, gather_shards(first, first))
    second, keep, send = call(
        functools.partial(second_kernel, rows_all),
        [shape, half_gram, half_gram],
        [SMEM, SMEM] + [VMEM] * (2 + len(terms)),
        [gram],
        name="second_filter",
    )(lower, upper, start, first, *terms)
    keep, other = sum_all(keep, send)
    basis = call(
        functools.partial(last_kernel, PIVOTS),
        jax.ShapeDtypeStruct((LANES + SIZE, rows), F32),
        [VMEM] * 3,
        [gram, gram],
        name="orthonormalize",
    )(keep, other, second)
    return basis.T


def solution(mesh):
    return jax.shard_map(
        per_device,
        mesh=mesh,
        in_specs=(
            P(("groups", "row"), None, "col"),
            P(("groups", "row"), "col"),
            P(("groups", "row", "col"), None),
            P("groups"),
            P("groups"),
        ),
        out_specs=P(("groups", "row", "col"), None),
        check_vma=False,
    )
```

```python
import functools

import jax
import jax.numpy as jnp
from jax import lax
from jax.experimental import pallas as pl
from jax.experimental.pallas import tpu as pltpu
from jax.sharding import PartitionSpec as P

LANES = 128
SIZE = LANES // 2
PIVOTS = 8
GIGA = 10**9
COSTS = ((3, 1, 3), (3, 1, 0))
F32 = jnp.float32
BF16 = jnp.bfloat16
VMEM = pl.BlockSpec(memory_space=pltpu.VMEM)
SMEM = pl.BlockSpec(memory_space=pltpu.SMEM)


def call(kernel, out_shape, in_specs, scratch=(), flops=1000, name=None):
    return pl.pallas_call(
        kernel,
        out_shape=out_shape,
        in_specs=in_specs,
        out_specs=jax.tree.map(lambda _: VMEM, out_shape),
        scratch_shapes=list(scratch),
        compiler_params=pltpu.CompilerParams(vmem_limit_bytes=40 * 1024 * 1024),
        cost_estimate=pl.CostEstimate(flops=flops, bytes_accessed=1000, transcendentals=0),
        name=name,
    )


def swap(x, axis, key):
    count = lax.axis_size(axis)
    return lax.ppermute(x, axis, [(i, i ^ key) for i in range(count)])


def gather_shards(own, twin):
    return list(zip(*(gather_one(*x) for x in zip(own, twin))))


def gather_one(own, twin):
    shards = {0: own}
    bit = lax.axis_size("row") // 2
    while bit:
        for key in list(shards):
            late = key == 0 and bit == 1
            shards[key | bit] = swap(twin if late else shards[key], "row", bit)
        bit //= 2
    return [shards[key] for key in range(len(shards))]


def pack_kernel(turned_ref, wide_out, thin_out):
    rows = turned_ref.shape[1]
    half = rows // 2
    turned = turned_ref[...].astype(F32)
    wide_out[...] = turned[:LANES].T.astype(BF16)
    thin = jnp.concatenate([turned[LANES:, :half], turned[LANES:, half:]], axis=0)
    thin_out[...] = thin.T.astype(BF16)


def load_kernel(own_blocks, orbitals, wide_ref, thin_ref, ids_ref, ham_ref, wide_out, thin_out, at_out):
    wide_out[...] = wide_ref[...]
    thin_out[...] = thin_ref[...]
    at_out[...] = (ids_ref[...] ^ (lax.axis_index("row") * own_blocks)) * orbitals


def product_kernel(keys, n_row, own_blocks, at_ref, ham_ref, *refs):
    wide, thin = refs[:n_row], refs[n_row : 2 * n_row]
    wide_out, thin_out = refs[2 * n_row : 2 * n_row + len(keys)], refs[2 * n_row + len(keys) : -1]
    source = refs[-1]
    orbitals = ham_ref.shape[1]
    rows = own_blocks * orbitals
    half = rows // 2
    me = lax.axis_index("col")
    first = [(key ^ me) * own_blocks for key in keys]
    low_lane = lax.broadcasted_iota(jnp.int32, (orbitals, LANES), 1) < SIZE
    for key in range(n_row):
        base = key * rows
        source[pl.ds(base, rows), pl.ds(0, LANES)] = wide[key][...]
        packed = thin[key][...]
        source[pl.ds(base, half), pl.ds(LANES, LANES)] = packed
        source[pl.ds(base + half, half), pl.ds(LANES, LANES)] = jnp.concatenate(
            [packed[:, SIZE:], packed[:, :SIZE]], axis=1
        )

    def term(i, block):
        picked = [
            source[pl.ds(pl.multiple_of(at_ref[slot, first[i] + block], orbitals), orbitals), :]
            for slot in range(at_ref.shape[0])
        ]
        return jnp.dot(
            ham_ref[first[i] + block],
            jnp.concatenate(picked, axis=0),
            preferred_element_type=F32,
        )

    for i in range(len(keys)):
        for block in range(own_blocks // 2):
            upper, lower = term(i, block), term(i, block + own_blocks // 2)
            at = pl.ds(block * orbitals, orbitals)
            wide_out[i][at, :] = upper[:, :LANES].astype(BF16)
            wide_out[i][pl.ds(half + block * orbitals, orbitals), :] = lower[:, :LANES].astype(BF16)
            turned = jnp.concatenate([lower[:, LANES + SIZE :], lower[:, LANES : LANES + SIZE]], axis=1)
            thin_out[i][at, :] = jnp.where(low_lane, upper[:, LANES:], turned).astype(BF16)


def product(keys, own_blocks, at, ham, parts):
    n_row = len(parts)
    orbitals = ham.shape[1]
    flops = 4 * own_blocks * len(keys) * orbitals * ham.shape[2] * LANES
    wide, thin = zip(*parts)
    outs = call(
        functools.partial(product_kernel, keys, n_row, own_blocks),
        [jax.ShapeDtypeStruct(x.shape, BF16) for x in parts[0] for _ in keys],
        [SMEM, VMEM] + [VMEM] * (2 * n_row),
        [pltpu.VMEM((own_blocks * n_row * orbitals, 2 * LANES), BF16)],
        flops=flops,
        name="product",
    )(at, ham, *wide, *thin)
    return list(zip(outs[: len(keys)], outs[len(keys) :]))


def add_kernel(a, b, *refs):
    count = len(refs) // 2
    refs[count][...] = (a[...].astype(F32) + b[...].astype(F32)).astype(BF16)
    for later, out in zip(refs[:count], refs[count + 1 :]):
        out[...] = later[...]


def add(a, b, *later, after=(), flops=1000):
    shapes = [jax.ShapeDtypeStruct(x.shape, BF16) for x in (a, *later)]
    count = len(after)
    kernel = lambda *refs: add_kernel(*refs[count:])
    specs = [VMEM] * (count + 2 + len(later))
    return call(kernel, shapes, specs, flops=flops, name="add")(*after, a, b, *later)


def partial_kernel(a, b, out):
    out[...] = a[...].astype(F32) + b[...].astype(F32)


def partial_sum(a, b, flops):
    shape = jax.ShapeDtypeStruct(a.shape, F32)
    return call(partial_kernel, shape, [VMEM] * 2, flops=flops, name="partial_sum")(a, b)


def summands(own_blocks, at, ham, parts, costs):
    n_col = lax.axis_size("col")
    if n_col != 4:
        terms = product(tuple(range(n_col)), own_blocks, at, ham, parts)
        sent = [[swap(x, "col", key) for x in terms[key]] for key in range(1, n_col)]
        return list(zip(terms[0], *sent))
    ((wide, thin),) = product((3,), own_blocks, at, ham, parts)
    wide, thin = swap(wide, "col", 1), swap(thin, "col", 1)
    across, near, own = product((2, 1, 0), own_blocks, at, ham, parts)
    (wide,) = add(across[0], wide)
    thin, *near = add(across[1], thin, *near, after=[wide], flops=costs[0] * GIGA + 1000)
    near = [swap(x, "col", 1) for x in near]
    across = [swap(x, "col", 2) for x in (wide, thin)]
    sums = [
        partial_sum(a, b, cost * GIGA + 1000) for a, b, cost in zip(own, across, costs[1:])
    ]
    return list(zip(sums, near))


def ends(lower_ref, upper_ref, shape):
    low = jnp.full(shape, lower_ref[0], F32)
    high = jnp.full(shape, upper_ref[0], F32)
    return (high + low) * 0.5, 1.0 / ((high - low) * 0.5)


def total_of(refs):
    acc = refs[0][...].astype(F32)
    for ref in refs[1:]:
        acc = acc + ref[...].astype(F32)
    return acc


def first_kernel(lower_ref, upper_ref, start, *refs):
    center, scale = ends(lower_ref, upper_ref, (1, LANES))
    moved = total_of(refs[:-1]) - center * start[...].astype(F32)
    refs[-1][...] = (moved * scale).astype(BF16)


def cross(a, b):
    return lax.dot_general(a, b, (((0,), (0,)), ((), ())), preferred_element_type=F32)


def second_kernel(rows_all, lower_ref, upper_ref, *refs):
    wide_out, thin_out, keep_out, send_out, gram = refs[-5:]
    count = (len(refs) - 5) // 2
    center, scale = ends(lower_ref, upper_ref, (1, LANES))
    for out, (start, first, *terms) in (
        (wide_out, refs[:count]),
        (thin_out, refs[count : 2 * count]),
    ):
        moved = total_of(terms) - center * first[...].astype(F32)
        out[...] = (2.0 * moved * scale - start[...].astype(F32)).astype(BF16)
    wide, thin = wide_out[...], thin_out[...]
    half = thin.shape[0]
    inv = 1.0 / rows_all
    aa = cross(wide, wide) * inv
    upper = cross(thin, wide[:half]) * inv
    lower = cross(thin, wide[half:]) * inv
    bb = cross(thin, thin) * inv
    turned = jnp.concatenate([bb[:SIZE, SIZE:], bb[:SIZE, :SIZE]], axis=1)
    low_lane = lax.broadcasted_iota(jnp.int32, (SIZE, LANES), 1) < SIZE
    gram[pl.ds(0, SIZE), :] = jnp.where(low_lane, aa[:SIZE], turned + bb[SIZE:])
    gram[pl.ds(SIZE, SIZE), :] = aa[SIZE:]
    gram[pl.ds(2 * SIZE, SIZE), :] = upper[:SIZE] + lower[SIZE:]
    part = 3 * SIZE // 2
    mine = lax.axis_index("row") & 1
    keep_out[...] = gram[pl.ds(pl.multiple_of(mine * part, 8), part), :]
    send_out[...] = gram[pl.ds(pl.multiple_of((1 - mine) * part, 8), part), :]


def inverse_factor(block, pivots):
    size = block.shape[0]
    tiles = size // 8
    rows = lax.broadcasted_iota(jnp.int32, (8, LANES), 0)
    lanes = lax.broadcasted_iota(jnp.int32, (8, LANES), 1)
    pad = jnp.concatenate([block, jnp.zeros((size, LANES - size), F32)], axis=1)
    a = [
        jnp.where(lanes == rows + (size + 8 * t), 1.0, pad[8 * t : 8 * t + 8]) for t in range(tiles)
    ]
    diag = [jnp.ones((8, LANES), F32) for _ in range(tiles)]
    full = (8, LANES)
    for j in range(0, size, pivots):
        t0, s0 = divmod(j, 8)
        cols = [
            [jnp.broadcast_to(a[t][:, j + k : j + k + 1], full) for t in range(t0, tiles)]
            for k in range(pivots)
        ]
        lines = [jnp.broadcast_to(a[t0][s0 + k : s0 + k + 1, :], full) for k in range(pivots)]
        small = [
            [jnp.broadcast_to(cols[q][0][s0 + k : s0 + k + 1, :], full) for q in range(k + 1)]
            for k in range(pivots)
        ]
        for k in range(pivots):
            d = small[k][k]
            diag[t0] = jnp.where(rows == s0 + k, d, diag[t0])
            r = 1.0 / d
            mult = {}
            for q in range(k + 1, pivots):
                mult[q] = small[q][k] * r
            for q in range(k + 1, pivots):
                lines[q] = lines[q] - mult[q] * lines[k]
                for p in range(k + 1, q + 1):
                    small[q][p] = small[q][p] - mult[q] * small[p][k]
            for i, t in enumerate(range(t0, tiles)):
                x = cols[k][i] * r
                if t == t0:
                    x = jnp.where(rows > s0 + k, x, 0.0)
                for q in range(k + 1, pivots):
                    cols[q][i] = cols[q][i] - cols[k][i] * mult[q]
                a[t] = a[t] - x * lines[k]
    out = jnp.concatenate([a[t] * lax.rsqrt(diag[t]) for t in range(tiles)], axis=0)
    return out[:, size:]


def last_kernel(pivots, keep_ref, other_ref, wide_ref, thin_ref, out_ref, gram, factor):
    size = LANES // 2
    part = 3 * size // 2
    mine = lax.axis_index("row") & 1
    gram[pl.ds(pl.multiple_of(mine * part, 8), part), :] = keep_ref[...]
    gram[pl.ds(pl.multiple_of((1 - mine) * part, 8), part), :] = other_ref[...]
    dot = functools.partial(
        jnp.dot, precision=lax.Precision.HIGHEST, preferred_element_type=F32
    )

    def dot_t(a, b):
        return lax.dot_general(
            a,
            b,
            (((1,), (1,)), ((), ())),
            precision=lax.Precision.HIGHEST,
            preferred_element_type=F32,
        )

    g00 = gram[pl.ds(0, size), :][:, :size]
    g22 = gram[pl.ds(0, size), :][:, size:]
    strip = gram[pl.ds(size, 2 * size), :]
    x0 = inverse_factor(g00, pivots)
    l_strip = dot_t(strip[:, :size], x0)
    rest = strip[:, size:] - dot_t(l_strip, l_strip[:size])
    x1 = inverse_factor(rest[:size], pivots)
    l10, l20 = l_strip[:size], l_strip[size:]
    l21 = dot_t(rest[size:], x1)
    x2 = inverse_factor(g22 - dot_t(l20, l20) - dot_t(l21, l21), pivots)
    n10 = -dot(x1, dot(l10, x0))
    n20 = -dot(x2, dot(l20, x0) + dot(l21, n10))
    n21 = -dot(x2, dot(l21, x1))
    zero = jnp.zeros((size, size), F32)
    factor[pl.ds(0, size), :] = jnp.concatenate([x0, zero], axis=1)
    factor[pl.ds(size, size), :] = jnp.concatenate([n10, x1], axis=1)
    factor[pl.ds(2 * size, size), :] = jnp.concatenate([n20, n21], axis=1)

    def apply(mat, vec):
        high = mat.astype(BF16)
        low = (mat - high.astype(F32)).astype(BF16)
        con = (((1,), (1,)), ((), ()))
        return lax.dot_general(high, vec, con, preferred_element_type=F32) + lax.dot_general(
            low, vec, con, preferred_element_type=F32
        )

    wide, thin = wide_ref[...], thin_ref[...]
    half = thin.shape[0]
    main = apply(factor[...], wide)
    out_ref[pl.ds(0, 2 * size), :] = main[: 2 * size]
    tail = jnp.concatenate(
        [
            apply(jnp.concatenate([x2, zero], axis=1), thin),
            apply(jnp.concatenate([zero, x2], axis=1), thin),
        ],
        axis=1,
    )
    out_ref[pl.ds(2 * size, size), :] = main[2 * size :] + tail


def sum_all(keep, send):
    acc = keep + swap(send, "row", 1)
    bit = 2
    while bit < lax.axis_size("row"):
        acc = acc + swap(acc, "row", bit)
        bit *= 2
    got = [swap(acc, "col", key) for key in range(1, lax.axis_size("col"))]
    for x in got:
        acc = acc + x
    return acc, swap(acc, "row", 1)


def per_device(hamiltonian, columns, vectors, lower, upper):
    rows = vectors.shape[0]
    orbitals = hamiltonian.shape[1]
    own_blocks = rows // orbitals
    rows_all = rows * lax.axis_size("col") * lax.axis_size("row")
    shapes = [jax.ShapeDtypeStruct((x, LANES), BF16) for x in (rows, rows // 2)]
    half_gram = jax.ShapeDtypeStruct((3 * SIZE // 2, LANES), F32)
    gram = pltpu.VMEM((3 * SIZE, LANES), F32)

    start = call(pack_kernel, shapes, [VMEM], name="pack")(vectors.T)
    *twin, at = call(
        functools.partial(load_kernel, own_blocks, orbitals),
        [*shapes, jax.ShapeDtypeStruct(columns.shape[::-1], jnp.int32)],
        [VMEM] * 4,
        name="load",
    )(*start, columns.T, hamiltonian)
    terms = summands(own_blocks, at, hamiltonian, gather_shards(start, twin), COSTS[0])
    first = [
        call(first_kernel, shape, [SMEM, SMEM] + [VMEM] * (1 + len(x)), name="first_filter")(
            lower, upper, vec, *x
        )
        for shape, vec, x in zip(shapes, start, terms)
    ]
    terms = summands(own_blocks, at, hamiltonian, gather_shards(first, first), COSTS[1])
    operands = [x for each in zip(start, first, terms) for x in (each[0], each[1], *each[2])]
    wide, thin, keep, send = call(
        functools.partial(second_kernel, rows_all),
        [*shapes, half_gram, half_gram],
        [SMEM, SMEM] + [VMEM] * len(operands),
        [gram],
        name="second_filter",
    )(lower, upper, *operands)
    keep, other = sum_all(keep, send)
    basis = call(
        functools.partial(last_kernel, PIVOTS),
        jax.ShapeDtypeStruct((LANES + SIZE, rows), F32),
        [VMEM] * 4,
        [gram, gram],
        name="orthonormalize",
    )(keep, other, wide, thin)
    return basis.T


def solution(mesh):
    return jax.shard_map(
        per_device,
        mesh=mesh,
        in_specs=(
            P(("groups", "row"), None, "col"),
            P(("groups", "row"), "col"),
            P(("groups", "row", "col"), None),
            P("groups"),
            P("groups"),
        ),
        out_specs=P(("groups", "row", "col"), None),
        check_vma=False,
    )
```

```python
import functools

import jax
import jax.numpy as jnp
from jax import lax
from jax.experimental import pallas as pl
from jax.experimental.pallas import tpu as pltpu
from jax.sharding import PartitionSpec as P

LANES = 128
SIZE = LANES // 2
GIGA = 10**9
COSTS = ((3, 1, 3), (3, 1, 0))
F32 = jnp.float32
BF16 = jnp.bfloat16
VMEM = pl.BlockSpec(memory_space=pltpu.VMEM)
SMEM = pl.BlockSpec(memory_space=pltpu.SMEM)


def call(kernel, out_shape, in_specs, scratch=(), flops=1000, name=None, out_specs=None):
    return pl.pallas_call(
        kernel,
        out_shape=out_shape,
        in_specs=in_specs,
        out_specs=out_specs or jax.tree.map(lambda _: VMEM, out_shape),
        scratch_shapes=list(scratch),
        compiler_params=pltpu.CompilerParams(vmem_limit_bytes=40 * 1024 * 1024),
        cost_estimate=pl.CostEstimate(flops=flops, bytes_accessed=1000, transcendentals=0),
        name=name,
    )


def swap(x, axis, key):
    count = lax.axis_size(axis)
    return lax.ppermute(x, axis, [(i, i ^ key) for i in range(count)])


def gather_shards(own, twin):
    return list(zip(*(gather_one(*x) for x in zip(own, twin))))


def gather_one(own, twin):
    shards = {0: own}
    bit = lax.axis_size("row") // 2
    while bit:
        for key in list(shards):
            late = key == 0 and bit == 1
            shards[key | bit] = swap(twin if late else shards[key], "row", bit)
        bit //= 2
    return [shards[key] for key in range(len(shards))]


def pack_kernel(turned_ref, wide_out, thin_out):
    rows = turned_ref.shape[1]
    half = rows // 2
    turned = turned_ref[...].astype(F32)
    wide_out[...] = turned[:LANES].T.astype(BF16)
    thin = jnp.concatenate([turned[LANES:, :half], turned[LANES:, half:]], axis=0)
    thin_out[...] = thin.T.astype(BF16)


def load_kernel(
    own_blocks,
    orbitals,
    lower_ref,
    upper_ref,
    wide_ref,
    thin_ref,
    ids_ref,
    ham_ref,
    wide_out,
    thin_out,
    at_out,
    ends_out,
):
    wide_out[...] = wide_ref[...]
    thin_out[...] = thin_ref[...]
    low = jnp.full((8, LANES), lower_ref[0], F32)
    high = jnp.full((8, LANES), upper_ref[0], F32)
    ends_out[pl.ds(0, 8), :] = (high + low) * 0.5
    ends_out[pl.ds(8, 8), :] = 1.0 / ((high - low) * 0.5)
    at_out[...] = (ids_ref[...] ^ (lax.axis_index("row") * own_blocks)) * orbitals


def product_kernel(keys, n_row, own_blocks, at_ref, ham_ref, *refs):
    wide, thin = refs[:n_row], refs[n_row : 2 * n_row]
    wide_out, thin_out = refs[2 * n_row : 2 * n_row + len(keys)], refs[2 * n_row + len(keys) : -1]
    source = refs[-1]
    orbitals = ham_ref.shape[1]
    rows = own_blocks * orbitals
    half = rows // 2
    me = lax.axis_index("col")
    first = [(key ^ me) * own_blocks for key in keys]
    low_lane = lax.broadcasted_iota(jnp.int32, (orbitals, LANES), 1) < SIZE
    for key in range(n_row):
        base = key * rows
        source[pl.ds(base, rows), pl.ds(0, LANES)] = wide[key][...]
        packed = thin[key][...]
        source[pl.ds(base, half), pl.ds(LANES, LANES)] = packed
        source[pl.ds(base + half, half), pl.ds(LANES, LANES)] = jnp.concatenate(
            [packed[:, SIZE:], packed[:, :SIZE]], axis=1
        )

    def term(i, block):
        picked = [
            source[pl.ds(pl.multiple_of(at_ref[slot, first[i] + block], orbitals), orbitals), :]
            for slot in range(at_ref.shape[0])
        ]
        return jnp.dot(
            ham_ref[first[i] + block],
            jnp.concatenate(picked, axis=0),
            preferred_element_type=F32,
        )

    for i in range(len(keys)):
        for block in range(own_blocks // 2):
            upper, lower = term(i, block), term(i, block + own_blocks // 2)
            at = pl.ds(block * orbitals, orbitals)
            wide_out[i][at, :] = upper[:, :LANES].astype(BF16)
            wide_out[i][pl.ds(half + block * orbitals, orbitals), :] = lower[:, :LANES].astype(BF16)
            turned = jnp.concatenate([lower[:, LANES + SIZE :], lower[:, LANES : LANES + SIZE]], axis=1)
            thin_out[i][at, :] = jnp.where(low_lane, upper[:, LANES:], turned).astype(BF16)


def product(keys, own_blocks, at, ham, parts):
    n_row = len(parts)
    orbitals = ham.shape[1]
    flops = 4 * own_blocks * len(keys) * orbitals * ham.shape[2] * LANES
    wide, thin = zip(*parts)
    outs = call(
        functools.partial(product_kernel, keys, n_row, own_blocks),
        [jax.ShapeDtypeStruct(x.shape, BF16) for x in parts[0] for _ in keys],
        [SMEM, VMEM] + [VMEM] * (2 * n_row),
        [pltpu.VMEM((own_blocks * n_row * orbitals, 2 * LANES), BF16)],
        flops=flops,
        name="product",
    )(at, ham, *wide, *thin)
    return list(zip(outs[: len(keys)], outs[len(keys) :]))


def add_kernel(a, b, *refs):
    count = len(refs) // 2
    refs[count][...] = (a[...].astype(F32) + b[...].astype(F32)).astype(BF16)
    for later, out in zip(refs[:count], refs[count + 1 :]):
        out[...] = later[...]


def add(a, b, *later, after=(), flops=1000):
    shapes = [jax.ShapeDtypeStruct(x.shape, BF16) for x in (a, *later)]
    count = len(after)
    kernel = lambda *refs: add_kernel(*refs[count:])
    specs = [VMEM] * (count + 2 + len(later))
    return call(kernel, shapes, specs, flops=flops, name="add")(*after, a, b, *later)


def partial_kernel(a, b, out):
    out[...] = a[...].astype(F32) + b[...].astype(F32)


def partial_sum(a, b, flops):
    shape = jax.ShapeDtypeStruct(a.shape, F32)
    return call(partial_kernel, shape, [VMEM] * 2, flops=flops, name="partial_sum")(a, b)


def summands(own_blocks, at, ham, parts, costs):
    n_col = lax.axis_size("col")
    if n_col != 4:
        terms = product(tuple(range(n_col)), own_blocks, at, ham, parts)
        sent = [[swap(x, "col", key) for x in terms[key]] for key in range(1, n_col)]
        return list(zip(terms[0], *sent))
    ((wide, thin),) = product((3,), own_blocks, at, ham, parts)
    wide, thin = swap(wide, "col", 1), swap(thin, "col", 1)
    across, near, own = product((2, 1, 0), own_blocks, at, ham, parts)
    (wide,) = add(across[0], wide)
    thin, *near = add(across[1], thin, *near, after=[wide], flops=costs[0] * GIGA + 1000)
    near = [swap(x, "col", 1) for x in near]
    across = [swap(x, "col", 2) for x in (wide, thin)]
    sums = [
        partial_sum(a, b, cost * GIGA + 1000) for a, b, cost in zip(own, across, costs[1:])
    ]
    return list(zip(sums, near))


def total_of(refs):
    acc = refs[0][...].astype(F32)
    for ref in refs[1:]:
        acc = acc + ref[...].astype(F32)
    return acc


def first_kernel(ends_ref, start, *refs):
    center, scale = ends_ref[pl.ds(0, 1), :], ends_ref[pl.ds(8, 1), :]
    moved = total_of(refs[:-1]) - center * start[...].astype(F32)
    refs[-1][...] = (moved * scale).astype(BF16)


def cross(a, b):
    return lax.dot_general(a, b, (((0,), (0,)), ((), ())), preferred_element_type=F32)


def second_kernel(rows_all, ends_ref, *refs):
    wide_out, thin_out, keep_out, send_out, gram = refs[-5:]
    count = (len(refs) - 5) // 2
    center, scale = ends_ref[pl.ds(0, 1), :], ends_ref[pl.ds(8, 1), :]
    for out, (start, first, *terms) in (
        (wide_out, refs[:count]),
        (thin_out, refs[count : 2 * count]),
    ):
        moved = total_of(terms) - center * first[...].astype(F32)
        out[...] = (2.0 * moved * scale - start[...].astype(F32)).astype(BF16)
    wide, thin = wide_out[...], thin_out[...]
    half = thin.shape[0]
    inv = 1.0 / rows_all
    aa = cross(wide, wide) * inv
    upper = cross(thin, wide[:half]) * inv
    lower = cross(thin, wide[half:]) * inv
    bb = cross(thin, thin) * inv
    turned = jnp.concatenate([bb[:SIZE, SIZE:], bb[:SIZE, :SIZE]], axis=1)
    low_lane = lax.broadcasted_iota(jnp.int32, (SIZE, LANES), 1) < SIZE
    gram[pl.ds(0, SIZE), :] = jnp.where(low_lane, aa[:SIZE], turned + bb[SIZE:])
    gram[pl.ds(SIZE, SIZE), :] = aa[SIZE:]
    gram[pl.ds(2 * SIZE, SIZE), :] = upper[:SIZE] + lower[SIZE:]
    part = 3 * SIZE // 2
    mine = lax.axis_index("row") & 1
    keep_out[...] = gram[pl.ds(pl.multiple_of(mine * part, 8), part), :]
    send_out[...] = gram[pl.ds(pl.multiple_of((1 - mine) * part, 8), part), :]


def inverse_factor(block):
    size = block.shape[0]
    tiles = size // 8
    rows = lax.broadcasted_iota(jnp.int32, (8, LANES), 0)
    lanes = lax.broadcasted_iota(jnp.int32, (8, LANES), 1)
    pad = jnp.concatenate([block, jnp.zeros((size, LANES - size), F32)], axis=1)
    a = [
        jnp.where(lanes == rows + (size + 8 * t), 1.0, pad[8 * t : 8 * t + 8]) for t in range(tiles)
    ]
    diag = [jnp.ones((8, LANES), F32) for _ in range(tiles)]
    full = (8, LANES)
    def row(x, at):
        return jnp.broadcast_to(x[at : at + 1, :], full)

    def column(x, at):
        return jnp.broadcast_to(x[:, at : at + 1], full)

    def corner(columns):
        return [[row(columns[q], k) for q in range(k + 1)] for k in range(8)]

    small = corner([column(a[0], k) for k in range(8)])
    for t0 in range(tiles):
        j = 8 * t0
        cols = [[column(a[t], j + k) for t in range(t0, tiles)] for k in range(8)]
        lines = [row(a[t0], k) for k in range(8)]
        ahead = t0 + 1 < tiles
        if ahead:
            later = corner([column(a[t0 + 1], j + 8 + k) for k in range(8)])
        for k in range(8):
            d = small[k][k]
            diag[t0] = jnp.where(rows == k, d, diag[t0])
            r = 1.0 / d
            mult = {q: small[q][k] * r for q in range(k + 1, 8)}
            for q in range(k + 1, 8):
                for p in range(k + 1, q + 1):
                    small[q][p] = small[q][p] - mult[q] * small[p][k]
            if ahead:
                below = [row(cols[k][1], q) for q in range(8)]
                for q in range(8):
                    scaled = below[q] * r
                    for p in range(q + 1):
                        later[q][p] = later[q][p] - scaled * below[p]
            for q in range(k + 1, 8):
                lines[q] = lines[q] - mult[q] * lines[k]
            for i, t in enumerate(range(t0, tiles)):
                x = cols[k][i] * r
                if t == t0:
                    x = jnp.where(rows > k, x, 0.0)
                for q in range(k + 1, 8):
                    cols[q][i] = cols[q][i] - cols[k][i] * mult[q]
                a[t] = a[t] - x * lines[k]
        if ahead:
            small = later
    out = jnp.concatenate([a[t] * lax.rsqrt(diag[t]) for t in range(tiles)], axis=0)
    return out[:, size:]


def last_kernel(keep_ref, other_ref, wide_ref, thin_ref, out_ref, gram, factor, result, sems):
    size = LANES // 2
    part = 3 * size // 2
    mine = lax.axis_index("row") & 1
    gram[pl.ds(pl.multiple_of(mine * part, 8), part), :] = keep_ref[...]
    gram[pl.ds(pl.multiple_of((1 - mine) * part, 8), part), :] = other_ref[...]
    dot = functools.partial(
        jnp.dot, precision=lax.Precision.HIGHEST, preferred_element_type=F32
    )

    def dot_t(a, b):
        return lax.dot_general(
            a,
            b,
            (((1,), (1,)), ((), ())),
            precision=lax.Precision.HIGHEST,
            preferred_element_type=F32,
        )

    g00 = gram[pl.ds(0, size), :][:, :size]
    g22 = gram[pl.ds(0, size), :][:, size:]
    strip = gram[pl.ds(size, 2 * size), :]
    x0 = inverse_factor(g00)
    l_strip = dot_t(strip[:, :size], x0)
    rest = strip[:, size:] - dot_t(l_strip, l_strip[:size])
    x1 = inverse_factor(rest[:size])
    l10, l20 = l_strip[:size], l_strip[size:]
    l21 = dot_t(rest[size:], x1)
    last = g22 - dot_t(l20, l20) - dot_t(l21, l21)
    n10 = -dot(x1, dot(l10, x0))
    below0 = dot(l20, x0) + dot(l21, n10)
    below1 = dot(l21, x1)
    zero = jnp.zeros((size, size), F32)
    factor[pl.ds(0, size), :] = jnp.concatenate([x0, zero], axis=1)
    factor[pl.ds(size, size), :] = jnp.concatenate([n10, x1], axis=1)

    def apply(mat, vec):
        high = mat.astype(BF16)
        low = (mat - high.astype(F32)).astype(BF16)
        con = (((1,), (1,)), ((), ()))
        return lax.dot_general(high, vec, con, preferred_element_type=F32) + lax.dot_general(
            low, vec, con, preferred_element_type=F32
        )

    wide, thin = wide_ref[...], thin_ref[...]
    half = thin.shape[0]
    head, foot = pl.ds(0, 2 * size), pl.ds(2 * size, size)
    result[head, :] = apply(factor[head, :], wide)
    early = pltpu.make_async_copy(result.at[head], out_ref.at[head], sems.at[0])
    early.start()
    x2 = inverse_factor(last)
    n20 = -dot(x2, below0)
    n21 = -dot(x2, below1)
    factor[foot, :] = jnp.concatenate([n20, n21], axis=1)
    tail = jnp.concatenate(
        [
            apply(jnp.concatenate([x2, zero], axis=1), thin),
            apply(jnp.concatenate([zero, x2], axis=1), thin),
        ],
        axis=1,
    )
    result[foot, :] = apply(factor[foot, :], wide) + tail
    late = pltpu.make_async_copy(result.at[foot], out_ref.at[foot], sems.at[1])
    late.start()
    early.wait()
    late.wait()


def sum_all(keep, send):
    acc = keep + swap(send, "row", 1)
    bit = 2
    while bit < lax.axis_size("row"):
        acc = acc + swap(acc, "row", bit)
        bit *= 2
    got = [swap(acc, "col", key) for key in range(1, lax.axis_size("col"))]
    for x in got:
        acc = acc + x
    return acc, swap(acc, "row", 1)


def per_device(hamiltonian, columns, vectors, lower, upper):
    rows = vectors.shape[0]
    orbitals = hamiltonian.shape[1]
    own_blocks = rows // orbitals
    rows_all = rows * lax.axis_size("col") * lax.axis_size("row")
    shapes = [jax.ShapeDtypeStruct((x, LANES), BF16) for x in (rows, rows // 2)]
    half_gram = jax.ShapeDtypeStruct((3 * SIZE // 2, LANES), F32)
    gram = pltpu.VMEM((3 * SIZE, LANES), F32)
    ends_shape = jax.ShapeDtypeStruct((16, LANES), F32)

    start = call(pack_kernel, shapes, [VMEM], name="pack")(vectors.T)
    *twin, at, ends = call(
        functools.partial(load_kernel, own_blocks, orbitals),
        [*shapes, jax.ShapeDtypeStruct(columns.shape[::-1], jnp.int32), ends_shape],
        [SMEM] * 2 + [VMEM] * 4,
        name="load",
    )(lower, upper, *start, columns.T, hamiltonian)
    terms = summands(own_blocks, at, hamiltonian, gather_shards(start, twin), COSTS[0])
    first = [
        call(first_kernel, shape, [VMEM] * (2 + len(x)), name="first_filter")(
            ends, vec, *x
        )
        for shape, vec, x in zip(shapes, start, terms)
    ]
    terms = summands(own_blocks, at, hamiltonian, gather_shards(first, first), COSTS[1])
    operands = [x for each in zip(start, first, terms) for x in (each[0], each[1], *each[2])]
    wide, thin, keep, send = call(
        functools.partial(second_kernel, rows_all),
        [*shapes, half_gram, half_gram],
        [VMEM] * (1 + len(operands)),
        [gram],
        name="second_filter",
    )(ends, *operands)
    keep, other = sum_all(keep, send)
    basis = call(
        last_kernel,
        jax.ShapeDtypeStruct((LANES + SIZE, rows), F32),
        [VMEM] * 4,
        [gram, gram, pltpu.VMEM((LANES + SIZE, rows), F32), pltpu.SemaphoreType.DMA((2,))],
        name="orthonormalize",
        out_specs=pl.BlockSpec(memory_space=pl.ANY),
    )(keep, other, wide, thin)
    return basis.T


def solution(mesh):
    return jax.shard_map(
        per_device,
        mesh=mesh,
        in_specs=(
            P(("groups", "row"), None, "col"),
            P(("groups", "row"), "col"),
            P(("groups", "row", "col"), None),
            P("groups"),
            P("groups"),
        ),
        out_specs=P(("groups", "row", "col"), None),
        check_vma=False,
    )
```

```python
import functools

import jax
import jax.numpy as jnp
from jax import lax
from jax.experimental import pallas as pl
from jax.experimental.pallas import tpu as pltpu
from jax.sharding import PartitionSpec as P

LANES = 128
SIZE = LANES // 2
GIGA = 10**9
COSTS = ((3, 1, 3), (3, 0, 0))
F32 = jnp.float32
BF16 = jnp.bfloat16
VMEM = pl.BlockSpec(memory_space=pltpu.VMEM)
SMEM = pl.BlockSpec(memory_space=pltpu.SMEM)


def call(kernel, out_shape, in_specs, scratch=(), flops=1000, name=None, out_specs=None):
    return pl.pallas_call(
        kernel,
        out_shape=out_shape,
        in_specs=in_specs,
        out_specs=out_specs or jax.tree.map(lambda _: VMEM, out_shape),
        scratch_shapes=list(scratch),
        compiler_params=pltpu.CompilerParams(vmem_limit_bytes=40 * 1024 * 1024),
        cost_estimate=pl.CostEstimate(flops=flops, bytes_accessed=1000, transcendentals=0),
        name=name,
    )


def swap(x, axis, key):
    count = lax.axis_size(axis)
    return lax.ppermute(x, axis, [(i, i ^ key) for i in range(count)])


def gather_one(own, twin):
    shards = {0: own}
    bit = lax.axis_size("row") // 2
    while bit:
        for key in list(shards):
            late = key == 0 and bit == 1
            shards[key | bit] = swap(twin if late else shards[key], "row", bit)
        bit //= 2
    return [shards[key] for key in range(len(shards))]


def pack_kernel(turned_ref, wide_out, thin_out):
    rows = turned_ref.shape[1]
    half = rows // 2
    turned = turned_ref[...].astype(F32)
    wide_out[...] = turned[:LANES].T.astype(BF16)
    thin = jnp.concatenate([turned[LANES:, :half], turned[LANES:, half:]], axis=0)
    thin_out[...] = thin.T.astype(BF16)


def load_kernel(
    own_blocks,
    orbitals,
    lower_ref,
    upper_ref,
    vec_ref,
    ids_ref,
    ham_ref,
    vec_out,
    at_out,
    ends_out,
):
    vec_out[...] = vec_ref[...]
    low = jnp.full((8, LANES), lower_ref[0], F32)
    high = jnp.full((8, LANES), upper_ref[0], F32)
    ends_out[pl.ds(0, 8), :] = (high + low) * 0.5
    ends_out[pl.ds(8, 8), :] = 1.0 / ((high - low) * 0.5)
    at_out[...] = (ids_ref[...] ^ (lax.axis_index("row") * own_blocks)) * orbitals


def product_kernel(keys, n_row, own_blocks, at_ref, ham_ref, *refs):
    wide, thin = refs[:n_row], refs[n_row : 2 * n_row]
    wide_out, thin_out = refs[2 * n_row : 2 * n_row + len(keys)], refs[2 * n_row + len(keys) : -1]
    source = refs[-1]
    orbitals = ham_ref.shape[1]
    rows = own_blocks * orbitals
    half = rows // 2
    me = lax.axis_index("col")
    first = [(key ^ me) * own_blocks for key in keys]
    low_lane = lax.broadcasted_iota(jnp.int32, (orbitals, LANES), 1) < SIZE
    for key in range(n_row):
        base = key * rows
        source[pl.ds(base, rows), pl.ds(0, LANES)] = wide[key][...]
        packed = thin[key][...]
        source[pl.ds(base, half), pl.ds(LANES, LANES)] = packed
        source[pl.ds(base + half, half), pl.ds(LANES, LANES)] = jnp.concatenate(
            [packed[:, SIZE:], packed[:, :SIZE]], axis=1
        )

    def term(i, block):
        picked = [
            source[pl.ds(pl.multiple_of(at_ref[slot, first[i] + block], orbitals), orbitals), :]
            for slot in range(at_ref.shape[0])
        ]
        return jnp.dot(
            ham_ref[first[i] + block],
            jnp.concatenate(picked, axis=0),
            preferred_element_type=F32,
        )

    for i in range(len(keys)):
        for block in range(own_blocks // 2):
            upper, lower = term(i, block), term(i, block + own_blocks // 2)
            at = pl.ds(block * orbitals, orbitals)
            wide_out[i][at, :] = upper[:, :LANES].astype(BF16)
            wide_out[i][pl.ds(half + block * orbitals, orbitals), :] = lower[:, :LANES].astype(BF16)
            turned = jnp.concatenate([lower[:, LANES + SIZE :], lower[:, LANES : LANES + SIZE]], axis=1)
            thin_out[i][at, :] = jnp.where(low_lane, upper[:, LANES:], turned).astype(BF16)


def product(keys, own_blocks, at, ham, parts):
    n_row = len(parts)
    orbitals = ham.shape[1]
    flops = 4 * own_blocks * len(keys) * orbitals * ham.shape[2] * LANES
    wide, thin = zip(*parts)
    outs = call(
        functools.partial(product_kernel, keys, n_row, own_blocks),
        [jax.ShapeDtypeStruct(x.shape, BF16) for x in parts[0] for _ in keys],
        [SMEM, VMEM] + [VMEM] * (2 * n_row),
        [pltpu.VMEM((own_blocks * n_row * orbitals, 2 * LANES), BF16)],
        flops=flops,
        name="product",
    )(at, ham, *wide, *thin)
    return list(zip(outs[: len(keys)], outs[len(keys) :]))


def add_kernel(a, b, *refs):
    count = len(refs) // 2
    refs[count][...] = (a[...].astype(F32) + b[...].astype(F32)).astype(BF16)
    for later, out in zip(refs[:count], refs[count + 1 :]):
        out[...] = later[...]


def add(a, b, *later, after=(), flops=1000):
    shapes = [jax.ShapeDtypeStruct(x.shape, BF16) for x in (a, *later)]
    count = len(after)
    kernel = lambda *refs: add_kernel(*refs[count:])
    specs = [VMEM] * (count + 2 + len(later))
    return call(kernel, shapes, specs, flops=flops, name="add")(*after, a, b, *later)


def partial_kernel(a, b, out):
    out[...] = a[...].astype(F32) + b[...].astype(F32)


def partial_sum(a, b, flops):
    shape = jax.ShapeDtypeStruct(a.shape, F32)
    return call(partial_kernel, shape, [VMEM] * 2, flops=flops, name="partial_sum")(a, b)


def summands(own_blocks, at, ham, parts, costs):
    n_col = lax.axis_size("col")
    if n_col != 4:
        terms = product(tuple(range(n_col)), own_blocks, at, ham, parts)
        sent = [[swap(x, "col", key) for x in terms[key]] for key in range(1, n_col)]
        return list(zip(terms[0], *sent))
    ((wide, thin),) = product((3,), own_blocks, at, ham, parts)
    wide, thin = swap(wide, "col", 1), swap(thin, "col", 1)
    across, near, own = product((2, 1, 0), own_blocks, at, ham, parts)
    (wide,) = add(across[0], wide)
    thin, *near = add(across[1], thin, *near, after=[wide], flops=costs[0] * GIGA + 1000)
    near = [swap(x, "col", 1) for x in near]
    across = [swap(x, "col", 2) for x in (wide, thin)]
    sums = [
        partial_sum(a, b, cost * GIGA + 1000) for a, b, cost in zip(own, across, costs[1:])
    ]
    return list(zip(sums, near))


def total_of(refs):
    acc = refs[0][...].astype(F32)
    for ref in refs[1:]:
        acc = acc + ref[...].astype(F32)
    return acc


def first_kernel(ends_ref, start, *refs):
    center, scale = ends_ref[pl.ds(0, 1), :], ends_ref[pl.ds(8, 1), :]
    moved = total_of(refs[:-1]) - center * start[...].astype(F32)
    refs[-1][...] = (moved * scale).astype(BF16)


def cross(a, b):
    return lax.dot_general(a, b, (((0,), (0,)), ((), ())), preferred_element_type=F32)


def second_kernel(rows_all, ends_ref, *refs):
    wide_out, thin_out, keep_out, send_out, gram = refs[-5:]
    count = (len(refs) - 5) // 2
    center, scale = ends_ref[pl.ds(0, 1), :], ends_ref[pl.ds(8, 1), :]
    for out, (start, first, *terms) in (
        (wide_out, refs[:count]),
        (thin_out, refs[count : 2 * count]),
    ):
        moved = total_of(terms) - center * first[...].astype(F32)
        out[...] = (2.0 * moved * scale - start[...].astype(F32)).astype(BF16)
    wide, thin = wide_out[...], thin_out[...]
    half = thin.shape[0]
    inv = 1.0 / rows_all
    aa = cross(wide, wide) * inv
    upper = cross(thin, wide[:half]) * inv
    lower = cross(thin, wide[half:]) * inv
    bb = cross(thin, thin) * inv
    turned = jnp.concatenate([bb[:SIZE, SIZE:], bb[:SIZE, :SIZE]], axis=1)
    low_lane = lax.broadcasted_iota(jnp.int32, (SIZE, LANES), 1) < SIZE
    gram[pl.ds(0, SIZE), :] = jnp.where(low_lane, aa[:SIZE], turned + bb[SIZE:])
    gram[pl.ds(SIZE, SIZE), :] = aa[SIZE:]
    gram[pl.ds(2 * SIZE, SIZE), :] = upper[:SIZE] + lower[SIZE:]
    part = 3 * SIZE // 2
    mine = lax.axis_index("row") & 1
    keep_out[...] = gram[pl.ds(pl.multiple_of(mine * part, 8), part), :]
    send_out[...] = gram[pl.ds(pl.multiple_of((1 - mine) * part, 8), part), :]


def inverse_factor(block):
    size = block.shape[0]
    tiles = size // 8
    rows = lax.broadcasted_iota(jnp.int32, (8, LANES), 0)
    lanes = lax.broadcasted_iota(jnp.int32, (8, LANES), 1)
    pad = jnp.concatenate([block, jnp.zeros((size, LANES - size), F32)], axis=1)
    a = [
        jnp.where(lanes == rows + (size + 8 * t), 1.0, pad[8 * t : 8 * t + 8]) for t in range(tiles)
    ]
    diag = [jnp.ones((8, LANES), F32) for _ in range(tiles)]
    full = (8, LANES)
    def row(x, at):
        return jnp.broadcast_to(x[at : at + 1, :], full)

    def column(x, at):
        return jnp.broadcast_to(x[:, at : at + 1], full)

    def corner(columns):
        return [[row(columns[q], k) for q in range(k + 1)] for k in range(8)]

    small = corner([column(a[0], k) for k in range(8)])
    for t0 in range(tiles):
        j = 8 * t0
        cols = [[column(a[t], j + k) for t in range(t0, tiles)] for k in range(8)]
        lines = [row(a[t0], k) for k in range(8)]
        ahead = t0 + 1 < tiles
        if ahead:
            later = corner([column(a[t0 + 1], j + 8 + k) for k in range(8)])
        for k in range(8):
            d = small[k][k]
            diag[t0] = jnp.where(rows == k, d, diag[t0])
            r = 1.0 / d
            mult = {q: small[q][k] * r for q in range(k + 1, 8)}
            for q in range(k + 1, 8):
                for p in range(k + 1, q + 1):
                    small[q][p] = small[q][p] - mult[q] * small[p][k]
            if ahead:
                below = [row(cols[k][1], q) for q in range(8)]
                for q in range(8):
                    scaled = below[q] * r
                    for p in range(q + 1):
                        later[q][p] = later[q][p] - scaled * below[p]
            for q in range(k + 1, 8):
                lines[q] = lines[q] - mult[q] * lines[k]
            for i, t in enumerate(range(t0, tiles)):
                x = cols[k][i] * r
                if t == t0:
                    x = jnp.where(rows > k, x, 0.0)
                for q in range(k + 1, 8):
                    cols[q][i] = cols[q][i] - cols[k][i] * mult[q]
                a[t] = a[t] - x * lines[k]
        if ahead:
            small = later
    out = jnp.concatenate([a[t] * lax.rsqrt(diag[t]) for t in range(tiles)], axis=0)
    return out[:, size:]


def last_kernel(keep_ref, other_ref, wide_ref, thin_ref, out_ref, gram, factor, result, sems):
    size = LANES // 2
    part = 3 * size // 2
    mine = lax.axis_index("row") & 1
    gram[pl.ds(pl.multiple_of(mine * part, 8), part), :] = keep_ref[...]
    gram[pl.ds(pl.multiple_of((1 - mine) * part, 8), part), :] = other_ref[...]
    dot = functools.partial(
        jnp.dot, precision=lax.Precision.HIGHEST, preferred_element_type=F32
    )

    def dot_t(a, b):
        return lax.dot_general(
            a,
            b,
            (((1,), (1,)), ((), ())),
            precision=lax.Precision.HIGHEST,
            preferred_element_type=F32,
        )

    g00 = gram[pl.ds(0, size), :][:, :size]
    g22 = gram[pl.ds(0, size), :][:, size:]
    strip = gram[pl.ds(size, 2 * size), :]
    x0 = inverse_factor(g00)
    l_strip = dot_t(strip[:, :size], x0)
    rest = strip[:, size:] - dot_t(l_strip, l_strip[:size])
    x1 = inverse_factor(rest[:size])
    l10, l20 = l_strip[:size], l_strip[size:]
    l21 = dot_t(rest[size:], x1)
    last = g22 - dot_t(l20, l20) - dot_t(l21, l21)
    n10 = -dot(x1, dot(l10, x0))
    below0 = dot(l20, x0) + dot(l21, n10)
    below1 = dot(l21, x1)
    zero = jnp.zeros((size, size), F32)
    factor[pl.ds(0, size), :] = jnp.concatenate([x0, zero], axis=1)
    factor[pl.ds(size, size), :] = jnp.concatenate([n10, x1], axis=1)

    def apply(mat, vec):
        high = mat.astype(BF16)
        low = (mat - high.astype(F32)).astype(BF16)
        con = (((1,), (1,)), ((), ()))
        return lax.dot_general(high, vec, con, preferred_element_type=F32) + lax.dot_general(
            low, vec, con, preferred_element_type=F32
        )

    wide, thin = wide_ref[...], thin_ref[...]
    half = thin.shape[0]
    head, foot = pl.ds(0, 2 * size), pl.ds(2 * size, size)
    result[head, :] = apply(factor[head, :], wide)
    early = pltpu.make_async_copy(result.at[head], out_ref.at[head], sems.at[0])
    early.start()
    x2 = inverse_factor(last)
    n20 = -dot(x2, below0)
    n21 = -dot(x2, below1)
    factor[foot, :] = jnp.concatenate([n20, n21], axis=1)
    tail = jnp.concatenate(
        [
            apply(jnp.concatenate([x2, zero], axis=1), thin),
            apply(jnp.concatenate([zero, x2], axis=1), thin),
        ],
        axis=1,
    )
    result[foot, :] = apply(factor[foot, :], wide) + tail
    late = pltpu.make_async_copy(result.at[foot], out_ref.at[foot], sems.at[1])
    late.start()
    early.wait()
    late.wait()


def sum_all(keep, send):
    acc = keep + swap(send, "row", 1)
    bit = 2
    while bit < lax.axis_size("row"):
        acc = acc + swap(acc, "row", bit)
        bit *= 2
    got = [swap(acc, "col", key) for key in range(1, lax.axis_size("col"))]
    for x in got:
        acc = acc + x
    return acc, swap(acc, "row", 1)


def per_device(hamiltonian, columns, vectors, lower, upper):
    rows = vectors.shape[0]
    orbitals = hamiltonian.shape[1]
    own_blocks = rows // orbitals
    rows_all = rows * lax.axis_size("col") * lax.axis_size("row")
    shapes = [jax.ShapeDtypeStruct((x, LANES), BF16) for x in (rows, rows // 2)]
    half_gram = jax.ShapeDtypeStruct((3 * SIZE // 2, LANES), F32)
    gram = pltpu.VMEM((3 * SIZE, LANES), F32)

    turned = vectors.T
    twin, at, ends = call(
        functools.partial(load_kernel, own_blocks, orbitals),
        [
            jax.ShapeDtypeStruct(turned.shape, BF16),
            jax.ShapeDtypeStruct(columns.shape[::-1], jnp.int32),
            jax.ShapeDtypeStruct((16, LANES), F32),
        ],
        [SMEM] * 2 + [VMEM] * 3,
        name="load",
    )(lower, upper, turned, columns.T, hamiltonian)
    parts = [
        call(pack_kernel, shapes, [VMEM], name="pack")(x) for x in gather_one(turned, twin)
    ]
    start = parts[0]
    terms = summands(own_blocks, at, hamiltonian, parts, COSTS[0])
    first = [
        call(first_kernel, shape, [VMEM] * (2 + len(x)), name="first_filter")(
            ends, vec, *x
        )
        for shape, vec, x in zip(shapes, start, terms)
    ]
    terms = summands(own_blocks, at, hamiltonian, list(zip(*(gather_one(x, x) for x in first))), COSTS[1])
    operands = [x for each in zip(start, first, terms) for x in (each[0], each[1], *each[2])]
    wide, thin, keep, send = call(
        functools.partial(second_kernel, rows_all),
        [*shapes, half_gram, half_gram],
        [VMEM] * (1 + len(operands)),
        [gram],
        name="second_filter",
    )(ends, *operands)
    keep, other = sum_all(keep, send)
    basis = call(
        last_kernel,
        jax.ShapeDtypeStruct((LANES + SIZE, rows), F32),
        [VMEM] * 4,
        [gram, gram, pltpu.VMEM((LANES + SIZE, rows), F32), pltpu.SemaphoreType.DMA((2,))],
        name="orthonormalize",
        out_specs=pl.BlockSpec(memory_space=pl.ANY),
    )(keep, other, wide, thin)
    return basis.T


def solution(mesh):
    return jax.shard_map(
        per_device,
        mesh=mesh,
        in_specs=(
            P(("groups", "row"), None, "col"),
            P(("groups", "row"), "col"),
            P(("groups", "row", "col"), None),
            P("groups"),
            P("groups"),
        ),
        out_specs=P(("groups", "row", "col"), None),
        check_vma=False,
    )
```

```python
import functools

import jax
import jax.numpy as jnp
from jax import lax
from jax.experimental import pallas as pl
from jax.experimental.pallas import tpu as pltpu
from jax.sharding import PartitionSpec as P

LANES = 128
SIZE = LANES // 2
GIGA = 10**9
COSTS = ((3, 1, 3), (3, 0, 0))
F32 = jnp.float32
BF16 = jnp.bfloat16
VMEM = pl.BlockSpec(memory_space=pltpu.VMEM)
SMEM = pl.BlockSpec(memory_space=pltpu.SMEM)


def call(kernel, out_shape, in_specs, scratch=(), flops=1000, name=None, out_specs=None):
    return pl.pallas_call(
        kernel,
        out_shape=out_shape,
        in_specs=in_specs,
        out_specs=out_specs or jax.tree.map(lambda _: VMEM, out_shape),
        scratch_shapes=list(scratch),
        compiler_params=pltpu.CompilerParams(vmem_limit_bytes=40 * 1024 * 1024),
        cost_estimate=pl.CostEstimate(flops=flops, bytes_accessed=1000, transcendentals=0),
        name=name,
    )


def swap(x, axis, key):
    count = lax.axis_size(axis)
    return lax.ppermute(x, axis, [(i, i ^ key) for i in range(count)])


def gather_one(own, twin):
    shards = {0: own}
    bit = lax.axis_size("row") // 2
    while bit:
        for key in list(shards):
            late = key == 0 and bit == 1
            shards[key | bit] = swap(twin if late else shards[key], "row", bit)
        bit //= 2
    return [shards[key] for key in range(len(shards))]


def pack_kernel(turned_ref, wide_out, thin_out):
    rows = turned_ref.shape[1]
    half = rows // 2
    turned = turned_ref[...].astype(F32)
    wide_out[...] = turned[:LANES].T.astype(BF16)
    thin = jnp.concatenate([turned[LANES:, :half], turned[LANES:, half:]], axis=0)
    thin_out[...] = thin.T.astype(BF16)


def load_kernel(
    own_blocks,
    orbitals,
    lower_ref,
    upper_ref,
    vec_ref,
    ids_ref,
    ham_ref,
    vec_out,
    at_out,
    ends_out,
):
    vec_out[...] = vec_ref[...]
    low = jnp.full((8, LANES), lower_ref[0], F32)
    high = jnp.full((8, LANES), upper_ref[0], F32)
    ends_out[pl.ds(0, 8), :] = (high + low) * 0.5
    ends_out[pl.ds(8, 8), :] = 1.0 / ((high - low) * 0.5)
    at_out[...] = (ids_ref[...] ^ (lax.axis_index("row") * own_blocks)) * orbitals


def product_kernel(keys, n_row, own_blocks, at_ref, ham_ref, *refs):
    wide, thin = refs[:n_row], refs[n_row : 2 * n_row]
    wide_out, thin_out = refs[2 * n_row : 2 * n_row + len(keys)], refs[2 * n_row + len(keys) : -1]
    source = refs[-1]
    orbitals = ham_ref.shape[1]
    rows = own_blocks * orbitals
    half = rows // 2
    me = lax.axis_index("col")
    first = [(key ^ me) * own_blocks for key in keys]
    low_lane = lax.broadcasted_iota(jnp.int32, (orbitals, LANES), 1) < SIZE
    for key in range(n_row):
        base = key * rows
        source[pl.ds(base, rows), pl.ds(0, LANES)] = wide[key][...]
        packed = thin[key][...]
        source[pl.ds(base, half), pl.ds(LANES, LANES)] = packed
        source[pl.ds(base + half, half), pl.ds(LANES, LANES)] = jnp.concatenate(
            [packed[:, SIZE:], packed[:, :SIZE]], axis=1
        )

    def term(i, block):
        picked = [
            source[pl.ds(pl.multiple_of(at_ref[slot, first[i] + block], orbitals), orbitals), :]
            for slot in range(at_ref.shape[0])
        ]
        return jnp.dot(
            ham_ref[first[i] + block],
            jnp.concatenate(picked, axis=0),
            preferred_element_type=F32,
        )

    for i in range(len(keys)):
        for block in range(own_blocks // 2):
            upper, lower = term(i, block), term(i, block + own_blocks // 2)
            at = pl.ds(block * orbitals, orbitals)
            wide_out[i][at, :] = upper[:, :LANES].astype(BF16)
            wide_out[i][pl.ds(half + block * orbitals, orbitals), :] = lower[:, :LANES].astype(BF16)
            turned = jnp.concatenate([lower[:, LANES + SIZE :], lower[:, LANES : LANES + SIZE]], axis=1)
            thin_out[i][at, :] = jnp.where(low_lane, upper[:, LANES:], turned).astype(BF16)


def product(keys, own_blocks, at, ham, parts):
    n_row = len(parts)
    orbitals = ham.shape[1]
    flops = 4 * own_blocks * len(keys) * orbitals * ham.shape[2] * LANES
    wide, thin = zip(*parts)
    outs = call(
        functools.partial(product_kernel, keys, n_row, own_blocks),
        [jax.ShapeDtypeStruct(x.shape, BF16) for x in parts[0] for _ in keys],
        [SMEM, VMEM] + [VMEM] * (2 * n_row),
        [pltpu.VMEM((own_blocks * n_row * orbitals, 2 * LANES), BF16)],
        flops=flops,
        name="product",
    )(at, ham, *wide, *thin)
    return list(zip(outs[: len(keys)], outs[len(keys) :]))


def add_kernel(a, b, *refs):
    count = len(refs) // 2
    refs[count][...] = (a[...].astype(F32) + b[...].astype(F32)).astype(BF16)
    for later, out in zip(refs[:count], refs[count + 1 :]):
        out[...] = later[...]


def add(a, b, *later, after=(), flops=1000):
    shapes = [jax.ShapeDtypeStruct(x.shape, BF16) for x in (a, *later)]
    count = len(after)
    kernel = lambda *refs: add_kernel(*refs[count:])
    specs = [VMEM] * (count + 2 + len(later))
    return call(kernel, shapes, specs, flops=flops, name="add")(*after, a, b, *later)


def partial_kernel(a, b, out):
    out[...] = a[...].astype(F32) + b[...].astype(F32)


def partial_sum(a, b, flops):
    shape = jax.ShapeDtypeStruct(a.shape, F32)
    return call(partial_kernel, shape, [VMEM] * 2, flops=flops, name="partial_sum")(a, b)


def summands(own_blocks, at, ham, parts, costs):
    n_col = lax.axis_size("col")
    if n_col != 4:
        terms = product(tuple(range(n_col)), own_blocks, at, ham, parts)
        sent = [[swap(x, "col", key) for x in terms[key]] for key in range(1, n_col)]
        return list(zip(terms[0], *sent))
    ((wide, thin),) = product((3,), own_blocks, at, ham, parts)
    wide, thin = swap(wide, "col", 1), swap(thin, "col", 1)
    across, near, own = product((2, 1, 0), own_blocks, at, ham, parts)
    (wide,) = add(across[0], wide)
    thin, *near = add(across[1], thin, *near, after=[wide], flops=costs[0] * GIGA + 1000)
    near = [swap(x, "col", 1) for x in near]
    across = [swap(x, "col", 2) for x in (wide, thin)]
    sums = [
        partial_sum(a, b, cost * GIGA + 1000) for a, b, cost in zip(own, across, costs[1:])
    ]
    return list(zip(sums, near))


def total_of(refs):
    acc = refs[0][...].astype(F32)
    for ref in refs[1:]:
        acc = acc + ref[...].astype(F32)
    return acc


def first_kernel(ends_ref, start, *refs):
    center, scale = ends_ref[pl.ds(0, 1), :], ends_ref[pl.ds(8, 1), :]
    moved = total_of(refs[:-1]) - center * start[...].astype(F32)
    refs[-1][...] = (moved * scale).astype(BF16)


def cross(a, b):
    return lax.dot_general(a, b, (((0,), (0,)), ((), ())), preferred_element_type=F32)


def second_kernel(rows_all, ends_ref, *refs):
    wide_out, thin_out, keep_out, send_out, gram = refs[-5:]
    count = (len(refs) - 5) // 2
    center, scale = ends_ref[pl.ds(0, 1), :], ends_ref[pl.ds(8, 1), :]
    for out, (start, first, *terms) in (
        (wide_out, refs[:count]),
        (thin_out, refs[count : 2 * count]),
    ):
        moved = total_of(terms) - center * first[...].astype(F32)
        out[...] = (2.0 * moved * scale - start[...].astype(F32)).astype(BF16)
    wide, thin = wide_out[...], thin_out[...]
    half = thin.shape[0]
    inv = 1.0 / rows_all
    aa = cross(wide, wide) * inv
    upper = cross(thin, wide[:half]) * inv
    lower = cross(thin, wide[half:]) * inv
    bb = cross(thin, thin) * inv
    bb = bb[:SIZE, :SIZE] + bb[SIZE:, SIZE:]
    corner = fold(aa[:SIZE, :SIZE])
    gram[pl.ds(0, SIZE // 2), :] = fold(bb)
    gram[pl.ds(SIZE // 2, SIZE), :] = aa[SIZE:]
    gram[pl.ds(3 * SIZE // 2, SIZE), :] = upper[:SIZE] + lower[SIZE:]
    part = gram.shape[0] // 2
    mine = lax.axis_index("row") & 1
    for out, half_at in ((keep_out, mine), (send_out, 1 - mine)):
        out[pl.ds(0, SIZE // 2), :] = corner
        out[pl.ds(SIZE // 2, part), :] = gram[pl.ds(pl.multiple_of(half_at * part, 8), part), :]


def fold(block):
    return jnp.concatenate([block[: SIZE // 2], block[SIZE // 2 :]], axis=1)


def unfold(rows):
    return jnp.concatenate([rows[:, :SIZE], rows[:, SIZE:]], axis=0)


def inverse_factor(block):
    size = block.shape[0]
    tiles = size // 8
    rows = lax.broadcasted_iota(jnp.int32, (8, LANES), 0)
    lanes = lax.broadcasted_iota(jnp.int32, (8, LANES), 1)
    pad = jnp.concatenate([block, jnp.zeros((size, LANES - size), F32)], axis=1)
    a = [
        jnp.where(lanes == rows + (size + 8 * t), 1.0, pad[8 * t : 8 * t + 8]) for t in range(tiles)
    ]
    diag = [jnp.ones((8, LANES), F32) for _ in range(tiles)]
    full = (8, LANES)
    def row(x, at):
        return jnp.broadcast_to(x[at : at + 1, :], full)

    def column(x, at):
        return jnp.broadcast_to(x[:, at : at + 1], full)

    def corner(columns):
        return [[row(columns[q], k) for q in range(k + 1)] for k in range(8)]

    small = corner([column(a[0], k) for k in range(8)])
    for t0 in range(tiles):
        j = 8 * t0
        cols = [[column(a[t], j + k) for t in range(t0, tiles)] for k in range(8)]
        lines = [row(a[t0], k) for k in range(8)]
        ahead = t0 + 1 < tiles
        if ahead:
            later = corner([column(a[t0 + 1], j + 8 + k) for k in range(8)])
        for k in range(8):
            d = small[k][k]
            diag[t0] = jnp.where(rows == k, d, diag[t0])
            r = 1.0 / d
            mult = {q: small[q][k] * r for q in range(k + 1, 8)}
            for q in range(k + 1, 8):
                for p in range(k + 1, q + 1):
                    small[q][p] = small[q][p] - mult[q] * small[p][k]
            if ahead:
                below = [row(cols[k][1], q) for q in range(8)]
                for q in range(8):
                    scaled = below[q] * r
                    for p in range(q + 1):
                        later[q][p] = later[q][p] - scaled * below[p]
            for q in range(k + 1, 8):
                lines[q] = lines[q] - mult[q] * lines[k]
            for i, t in enumerate(range(t0, tiles)):
                x = cols[k][i] * r
                if t == t0:
                    x = jnp.where(rows > k, x, 0.0)
                for q in range(k + 1, 8):
                    cols[q][i] = cols[q][i] - cols[k][i] * mult[q]
                a[t] = a[t] - x * lines[k]
        if ahead:
            small = later
    out = jnp.concatenate([a[t] * lax.rsqrt(diag[t]) for t in range(tiles)], axis=0)
    return out[:, size:]


def corner_kernel(keep_ref, out_ref):
    out_ref[...] = inverse_factor(unfold(keep_ref[pl.ds(0, SIZE // 2), :]))


def last_kernel(
    keep_ref, other_ref, corner_ref, wide_ref, thin_ref, out_ref, gram, factor, result, sems
):
    size = LANES // 2
    part = gram.shape[0] // 2
    mine = lax.axis_index("row") & 1
    for ref, half_at in ((keep_ref, mine), (other_ref, 1 - mine)):
        gram[pl.ds(pl.multiple_of(half_at * part, 8), part), :] = ref[pl.ds(size // 2, part), :]
    dot = functools.partial(
        jnp.dot, precision=lax.Precision.HIGHEST, preferred_element_type=F32
    )

    def dot_t(a, b):
        return lax.dot_general(
            a,
            b,
            (((1,), (1,)), ((), ())),
            precision=lax.Precision.HIGHEST,
            preferred_element_type=F32,
        )

    g22 = unfold(gram[pl.ds(0, size // 2), :])
    strip = gram[pl.ds(size // 2, 2 * size), :]
    x0 = corner_ref[...]
    l_strip = dot_t(strip[:, :size], x0)
    rest = strip[:, size:] - dot_t(l_strip, l_strip[:size])
    x1 = inverse_factor(rest[:size])
    l10, l20 = l_strip[:size], l_strip[size:]
    l21 = dot_t(rest[size:], x1)
    last = g22 - dot_t(l20, l20) - dot_t(l21, l21)
    n10 = -dot(x1, dot(l10, x0))
    below0 = dot(l20, x0) + dot(l21, n10)
    below1 = dot(l21, x1)
    zero = jnp.zeros((size, size), F32)
    factor[pl.ds(0, size), :] = jnp.concatenate([x0, zero], axis=1)
    factor[pl.ds(size, size), :] = jnp.concatenate([n10, x1], axis=1)

    def apply(mat, vec):
        high = mat.astype(BF16)
        low = (mat - high.astype(F32)).astype(BF16)
        con = (((1,), (1,)), ((), ()))
        return lax.dot_general(high, vec, con, preferred_element_type=F32) + lax.dot_general(
            low, vec, con, preferred_element_type=F32
        )

    wide, thin = wide_ref[...], thin_ref[...]
    half = thin.shape[0]
    head, foot = pl.ds(0, 2 * size), pl.ds(2 * size, size)
    result[head, :] = apply(factor[head, :], wide)
    early = pltpu.make_async_copy(result.at[head], out_ref.at[head], sems.at[0])
    early.start()
    x2 = inverse_factor(last)
    n20 = -dot(x2, below0)
    n21 = -dot(x2, below1)
    factor[foot, :] = jnp.concatenate([n20, n21], axis=1)
    tail = jnp.concatenate(
        [
            apply(jnp.concatenate([x2, zero], axis=1), thin),
            apply(jnp.concatenate([zero, x2], axis=1), thin),
        ],
        axis=1,
    )
    result[foot, :] = apply(factor[foot, :], wide) + tail
    late = pltpu.make_async_copy(result.at[foot], out_ref.at[foot], sems.at[1])
    late.start()
    early.wait()
    late.wait()


def sum_all(keep, send):
    acc = keep + swap(send, "row", 1)
    bit = 2
    while bit < lax.axis_size("row"):
        acc = acc + swap(acc, "row", bit)
        bit *= 2
    got = [swap(acc, "col", key) for key in range(1, lax.axis_size("col"))]
    for x in got:
        acc = acc + x
    return acc, swap(acc, "row", 1)


def per_device(hamiltonian, columns, vectors, lower, upper):
    rows = vectors.shape[0]
    orbitals = hamiltonian.shape[1]
    own_blocks = rows // orbitals
    rows_all = rows * lax.axis_size("col") * lax.axis_size("row")
    shapes = [jax.ShapeDtypeStruct((x, LANES), BF16) for x in (rows, rows // 2)]
    half_gram = jax.ShapeDtypeStruct((7 * SIZE // 4, LANES), F32)
    gram = pltpu.VMEM((5 * SIZE // 2, LANES), F32)
    factor = pltpu.VMEM((3 * SIZE, LANES), F32)

    turned = vectors.T
    twin, at, ends = call(
        functools.partial(load_kernel, own_blocks, orbitals),
        [
            jax.ShapeDtypeStruct(turned.shape, BF16),
            jax.ShapeDtypeStruct(columns.shape[::-1], jnp.int32),
            jax.ShapeDtypeStruct((16, LANES), F32),
        ],
        [SMEM] * 2 + [VMEM] * 3,
        name="load",
    )(lower, upper, turned, columns.T, hamiltonian)
    parts = [
        call(pack_kernel, shapes, [VMEM], name="pack")(x) for x in gather_one(turned, twin)
    ]
    start = parts[0]
    terms = summands(own_blocks, at, hamiltonian, parts, COSTS[0])
    first = [
        call(first_kernel, shape, [VMEM] * (2 + len(x)), name="first_filter")(
            ends, vec, *x
        )
        for shape, vec, x in zip(shapes, start, terms)
    ]
    terms = summands(own_blocks, at, hamiltonian, list(zip(*(gather_one(x, x) for x in first))), COSTS[1])
    operands = [x for each in zip(start, first, terms) for x in (each[0], each[1], *each[2])]
    wide, thin, keep, send = call(
        functools.partial(second_kernel, rows_all),
        [*shapes, half_gram, half_gram],
        [VMEM] * (1 + len(operands)),
        [gram],
        name="second_filter",
    )(ends, *operands)
    keep, other = sum_all(keep, send)
    corner = call(
        corner_kernel, jax.ShapeDtypeStruct((SIZE, SIZE), F32), [VMEM], flops=10**9, name="corner"
    )(keep)
    basis = call(
        last_kernel,
        jax.ShapeDtypeStruct((LANES + SIZE, rows), F32),
        [VMEM] * 5,
        [gram, factor, pltpu.VMEM((LANES + SIZE, rows), F32), pltpu.SemaphoreType.DMA((2,))],
        name="orthonormalize",
        out_specs=pl.BlockSpec(memory_space=pl.ANY),
    )(keep, other, corner, wide, thin)
    return basis.T


def solution(mesh):
    return jax.shard_map(
        per_device,
        mesh=mesh,
        in_specs=(
            P(("groups", "row"), None, "col"),
            P(("groups", "row"), "col"),
            P(("groups", "row", "col"), None),
            P("groups"),
            P("groups"),
        ),
        out_specs=P(("groups", "row", "col"), None),
        check_vma=False,
    )
```

```python
import functools

import jax
import jax.numpy as jnp
from jax import lax
from jax.experimental import pallas as pl
from jax.experimental.pallas import tpu as pltpu
from jax.sharding import PartitionSpec as P

LANES = 128
SIZE = LANES // 2
GIGA = 10**9
COSTS = ((3, 1, 3), (3, 0, 0))
F32 = jnp.float32
BF16 = jnp.bfloat16
VMEM = pl.BlockSpec(memory_space=pltpu.VMEM)
SMEM = pl.BlockSpec(memory_space=pltpu.SMEM)


def call(kernel, out_shape, in_specs, scratch=(), flops=1000, name=None, out_specs=None):
    return pl.pallas_call(
        kernel,
        out_shape=out_shape,
        in_specs=in_specs,
        out_specs=out_specs or jax.tree.map(lambda _: VMEM, out_shape),
        scratch_shapes=list(scratch),
        compiler_params=pltpu.CompilerParams(vmem_limit_bytes=40 * 1024 * 1024),
        cost_estimate=pl.CostEstimate(flops=flops, bytes_accessed=1000, transcendentals=0),
        name=name,
    )


def swap(x, axis, key):
    count = lax.axis_size(axis)
    return lax.ppermute(x, axis, [(i, i ^ key) for i in range(count)])


def gather_one(own, twin):
    shards = {0: own}
    bit = lax.axis_size("row") // 2
    while bit:
        for key in list(shards):
            late = key == 0 and bit == 1
            shards[key | bit] = swap(twin if late else shards[key], "row", bit)
        bit //= 2
    return [shards[key] for key in range(len(shards))]


def pack_kernel(turned_ref, wide_out, thin_out):
    rows = turned_ref.shape[1]
    half = rows // 2
    turned = turned_ref[...].astype(F32)
    wide_out[...] = turned[:LANES].T.astype(BF16)
    thin = jnp.concatenate([turned[LANES:, :half], turned[LANES:, half:]], axis=0)
    thin_out[...] = thin.T.astype(BF16)


def load_kernel(
    own_blocks,
    orbitals,
    lower_ref,
    upper_ref,
    vec_ref,
    ids_ref,
    ham_ref,
    vec_out,
    at_out,
    ends_out,
):
    vec_out[...] = vec_ref[...]
    low = jnp.full((8, LANES), lower_ref[0], F32)
    high = jnp.full((8, LANES), upper_ref[0], F32)
    ends_out[pl.ds(0, 8), :] = (high + low) * 0.5
    ends_out[pl.ds(8, 8), :] = 1.0 / ((high - low) * 0.5)
    at_out[...] = (ids_ref[...] ^ (lax.axis_index("row") * own_blocks)) * orbitals


def product_kernel(keys, n_row, own_blocks, at_vmem, ham_ref, *refs):
    wide, thin = refs[:n_row], refs[n_row : 2 * n_row]
    wide_out, thin_out = refs[2 * n_row : 2 * n_row + len(keys)], refs[2 * n_row + len(keys) : -3]
    source, at_ref, sem = refs[-3:]
    copy = pltpu.make_async_copy(at_vmem, at_ref, sem)
    copy.start()
    orbitals = ham_ref.shape[1]
    rows = own_blocks * orbitals
    half = rows // 2
    me = lax.axis_index("col")
    first = [(key ^ me) * own_blocks for key in keys]
    low_lane = lax.broadcasted_iota(jnp.int32, (orbitals, LANES), 1) < SIZE
    for key in range(n_row):
        base = key * rows
        source[pl.ds(base, rows), pl.ds(0, LANES)] = wide[key][...]
        packed = thin[key][...]
        source[pl.ds(base, half), pl.ds(LANES, LANES)] = packed
        source[pl.ds(base + half, half), pl.ds(LANES, LANES)] = jnp.concatenate(
            [packed[:, SIZE:], packed[:, :SIZE]], axis=1
        )

    copy.wait()

    def term(i, block):
        picked = [
            source[pl.ds(pl.multiple_of(at_ref[slot, first[i] + block], orbitals), orbitals), :]
            for slot in range(at_ref.shape[0])
        ]
        return jnp.dot(
            ham_ref[first[i] + block],
            jnp.concatenate(picked, axis=0),
            preferred_element_type=F32,
        )

    for i in range(len(keys)):
        for block in range(own_blocks // 2):
            upper, lower = term(i, block), term(i, block + own_blocks // 2)
            at = pl.ds(block * orbitals, orbitals)
            wide_out[i][at, :] = upper[:, :LANES].astype(BF16)
            wide_out[i][pl.ds(half + block * orbitals, orbitals), :] = lower[:, :LANES].astype(BF16)
            turned = jnp.concatenate([lower[:, LANES + SIZE :], lower[:, LANES : LANES + SIZE]], axis=1)
            thin_out[i][at, :] = jnp.where(low_lane, upper[:, LANES:], turned).astype(BF16)


def product(keys, own_blocks, at, ham, parts):
    n_row = len(parts)
    orbitals = ham.shape[1]
    flops = 4 * own_blocks * len(keys) * orbitals * ham.shape[2] * LANES
    wide, thin = zip(*parts)
    outs = call(
        functools.partial(product_kernel, keys, n_row, own_blocks),
        [jax.ShapeDtypeStruct(x.shape, BF16) for x in parts[0] for _ in keys],
        [VMEM, VMEM] + [VMEM] * (2 * n_row),
        [
            pltpu.VMEM((own_blocks * n_row * orbitals, 2 * LANES), BF16),
            pltpu.SMEM(at.shape, jnp.int32),
            pltpu.SemaphoreType.DMA,
        ],
        flops=flops,
        name="product",
    )(at, ham, *wide, *thin)
    return list(zip(outs[: len(keys)], outs[len(keys) :]))


def add_kernel(a, b, *refs):
    count = len(refs) // 2
    refs[count][...] = (a[...].astype(F32) + b[...].astype(F32)).astype(BF16)
    for later, out in zip(refs[:count], refs[count + 1 :]):
        out[...] = later[...]


def add(a, b, *later, after=(), flops=1000):
    shapes = [jax.ShapeDtypeStruct(x.shape, BF16) for x in (a, *later)]
    count = len(after)
    kernel = lambda *refs: add_kernel(*refs[count:])
    specs = [VMEM] * (count + 2 + len(later))
    return call(kernel, shapes, specs, flops=flops, name="add")(*after, a, b, *later)


def partial_kernel(a, b, out):
    out[...] = a[...].astype(F32) + b[...].astype(F32)


def partial_sum(a, b, flops):
    shape = jax.ShapeDtypeStruct(a.shape, F32)
    return call(partial_kernel, shape, [VMEM] * 2, flops=flops, name="partial_sum")(a, b)


def summands(own_blocks, at, ham, parts, costs):
    n_col = lax.axis_size("col")
    if n_col != 4:
        terms = product(tuple(range(n_col)), own_blocks, at, ham, parts)
        sent = [[swap(x, "col", key) for x in terms[key]] for key in range(1, n_col)]
        return list(zip(terms[0], *sent))
    ((wide, thin),) = product((3,), own_blocks, at, ham, parts)
    wide, thin = swap(wide, "col", 1), swap(thin, "col", 1)
    across, near, own = product((2, 1, 0), own_blocks, at, ham, parts)
    (wide,) = add(across[0], wide)
    thin, *near = add(across[1], thin, *near, after=[wide], flops=costs[0] * GIGA + 1000)
    near = [swap(x, "col", 1) for x in near]
    across = [swap(x, "col", 2) for x in (wide, thin)]
    sums = [
        partial_sum(a, b, cost * GIGA + 1000) for a, b, cost in zip(own, across, costs[1:])
    ]
    return list(zip(sums, near))


def total_of(refs):
    acc = refs[0][...].astype(F32)
    for ref in refs[1:]:
        acc = acc + ref[...].astype(F32)
    return acc


def first_kernel(ends_ref, start, *refs):
    center, scale = ends_ref[pl.ds(0, 1), :], ends_ref[pl.ds(8, 1), :]
    moved = total_of(refs[:-1]) - center * start[...].astype(F32)
    refs[-1][...] = (moved * scale).astype(BF16)


def cross(a, b):
    return lax.dot_general(a, b, (((0,), (0,)), ((), ())), preferred_element_type=F32)


def second_kernel(rows_all, ends_ref, *refs):
    wide_out, thin_out, keep_out, send_out, gram = refs[-5:]
    count = (len(refs) - 5) // 2
    center, scale = ends_ref[pl.ds(0, 1), :], ends_ref[pl.ds(8, 1), :]
    for out, (start, first, *terms) in (
        (wide_out, refs[:count]),
        (thin_out, refs[count : 2 * count]),
    ):
        moved = total_of(terms) - center * first[...].astype(F32)
        out[...] = (2.0 * moved * scale - start[...].astype(F32)).astype(BF16)
    wide, thin = wide_out[...], thin_out[...]
    half = thin.shape[0]
    inv = 1.0 / rows_all
    aa = cross(wide, wide) * inv
    upper = cross(thin, wide[:half]) * inv
    lower = cross(thin, wide[half:]) * inv
    bb = cross(thin, thin) * inv
    bb = bb[:SIZE, :SIZE] + bb[SIZE:, SIZE:]
    corner = fold(aa[:SIZE, :SIZE])
    gram[pl.ds(0, SIZE // 2), :] = fold(bb)
    gram[pl.ds(SIZE // 2, SIZE), :] = aa[SIZE:]
    gram[pl.ds(3 * SIZE // 2, SIZE), :] = upper[:SIZE] + lower[SIZE:]
    part = gram.shape[0] // 2
    mine = lax.axis_index("row") & 1
    for out, half_at in ((keep_out, mine), (send_out, 1 - mine)):
        out[pl.ds(0, SIZE // 2), :] = corner
        out[pl.ds(SIZE // 2, part), :] = gram[pl.ds(pl.multiple_of(half_at * part, 8), part), :]


def fold(block):
    return jnp.concatenate([block[: SIZE // 2], block[SIZE // 2 :]], axis=1)


def unfold(rows):
    return jnp.concatenate([rows[:, :SIZE], rows[:, SIZE:]], axis=0)


def inverse_factor(block):
    size = block.shape[0]
    tiles = size // 8
    rows = lax.broadcasted_iota(jnp.int32, (8, LANES), 0)
    lanes = lax.broadcasted_iota(jnp.int32, (8, LANES), 1)
    pad = jnp.concatenate([block, jnp.zeros((size, LANES - size), F32)], axis=1)
    a = [
        jnp.where(lanes == rows + (size + 8 * t), 1.0, pad[8 * t : 8 * t + 8]) for t in range(tiles)
    ]
    diag = [jnp.ones((8, LANES), F32) for _ in range(tiles)]
    full = (8, LANES)
    def row(x, at):
        return jnp.broadcast_to(x[at : at + 1, :], full)

    def column(x, at):
        return jnp.broadcast_to(x[:, at : at + 1], full)

    def corner(columns):
        return [[row(columns[q], k) for q in range(k + 1)] for k in range(8)]

    small = corner([column(a[0], k) for k in range(8)])
    for t0 in range(tiles):
        j = 8 * t0
        cols = [[column(a[t], j + k) for t in range(t0, tiles)] for k in range(8)]
        lines = [row(a[t0], k) for k in range(8)]
        ahead = t0 + 1 < tiles
        if ahead:
            later = corner([column(a[t0 + 1], j + 8 + k) for k in range(8)])
        for k in range(8):
            d = small[k][k]
            diag[t0] = jnp.where(rows == k, d, diag[t0])
            r = 1.0 / d
            mult = {q: small[q][k] * r for q in range(k + 1, 8)}
            for q in range(k + 1, 8):
                for p in range(k + 1, q + 1):
                    small[q][p] = small[q][p] - mult[q] * small[p][k]
            if ahead:
                below = [row(cols[k][1], q) for q in range(8)]
                for q in range(8):
                    scaled = below[q] * r
                    for p in range(q + 1):
                        later[q][p] = later[q][p] - scaled * below[p]
            for q in range(k + 1, 8):
                lines[q] = lines[q] - mult[q] * lines[k]
            for i, t in enumerate(range(t0, tiles)):
                x = cols[k][i] * r
                if t == t0:
                    x = jnp.where(rows > k, x, 0.0)
                for q in range(k + 1, 8):
                    cols[q][i] = cols[q][i] - cols[k][i] * mult[q]
                a[t] = a[t] - x * lines[k]
        if ahead:
            small = later
    out = jnp.concatenate([a[t] * lax.rsqrt(diag[t]) for t in range(tiles)], axis=0)
    return out[:, size:]


def corner_kernel(keep_ref, out_ref):
    out_ref[...] = inverse_factor(unfold(keep_ref[pl.ds(0, SIZE // 2), :]))


def last_kernel(
    keep_ref, other_ref, corner_ref, wide_ref, thin_ref, out_ref, gram, factor, result, sems
):
    size = LANES // 2
    part = gram.shape[0] // 2
    mine = lax.axis_index("row") & 1
    for ref, half_at in ((keep_ref, mine), (other_ref, 1 - mine)):
        gram[pl.ds(pl.multiple_of(half_at * part, 8), part), :] = ref[pl.ds(size // 2, part), :]
    dot = functools.partial(
        jnp.dot, precision=lax.Precision.HIGHEST, preferred_element_type=F32
    )

    def dot_t(a, b):
        return lax.dot_general(
            a,
            b,
            (((1,), (1,)), ((), ())),
            precision=lax.Precision.HIGHEST,
            preferred_element_type=F32,
        )

    g22 = unfold(gram[pl.ds(0, size // 2), :])
    strip = gram[pl.ds(size // 2, 2 * size), :]
    x0 = corner_ref[...]
    l_strip = dot_t(strip[:, :size], x0)
    rest = strip[:, size:] - dot_t(l_strip, l_strip[:size])
    x1 = inverse_factor(rest[:size])
    l10, l20 = l_strip[:size], l_strip[size:]
    l21 = dot_t(rest[size:], x1)
    last = g22 - dot_t(l20, l20) - dot_t(l21, l21)
    n10 = -dot(x1, dot(l10, x0))
    below0 = dot(l20, x0) + dot(l21, n10)
    below1 = dot(l21, x1)
    zero = jnp.zeros((size, size), F32)
    factor[pl.ds(0, size), :] = jnp.concatenate([x0, zero], axis=1)
    factor[pl.ds(size, size), :] = jnp.concatenate([n10, x1], axis=1)

    def apply(mat, vec):
        high = mat.astype(BF16)
        low = (mat - high.astype(F32)).astype(BF16)
        con = (((1,), (1,)), ((), ()))
        return lax.dot_general(high, vec, con, preferred_element_type=F32) + lax.dot_general(
            low, vec, con, preferred_element_type=F32
        )

    wide, thin = wide_ref[...], thin_ref[...]
    half = thin.shape[0]
    head, foot = pl.ds(0, 2 * size), pl.ds(2 * size, size)
    result[head, :] = apply(factor[head, :], wide)
    early = pltpu.make_async_copy(result.at[head], out_ref.at[head], sems.at[0])
    early.start()
    x2 = inverse_factor(last)
    n20 = -dot(x2, below0)
    n21 = -dot(x2, below1)
    factor[foot, :] = jnp.concatenate([n20, n21], axis=1)
    tail = jnp.concatenate(
        [
            apply(jnp.concatenate([x2, zero], axis=1), thin),
            apply(jnp.concatenate([zero, x2], axis=1), thin),
        ],
        axis=1,
    )
    result[foot, :] = apply(factor[foot, :], wide) + tail
    late = pltpu.make_async_copy(result.at[foot], out_ref.at[foot], sems.at[1])
    late.start()
    early.wait()
    late.wait()


def sum_all(keep, send):
    acc = keep + swap(send, "row", 1)
    bit = 2
    while bit < lax.axis_size("row"):
        acc = acc + swap(acc, "row", bit)
        bit *= 2
    got = [swap(acc, "col", key) for key in range(1, lax.axis_size("col"))]
    for x in got:
        acc = acc + x
    return acc, swap(acc, "row", 1)


def per_device(hamiltonian, columns, vectors, lower, upper):
    rows = vectors.shape[0]
    orbitals = hamiltonian.shape[1]
    own_blocks = rows // orbitals
    rows_all = rows * lax.axis_size("col") * lax.axis_size("row")
    shapes = [jax.ShapeDtypeStruct((x, LANES), BF16) for x in (rows, rows // 2)]
    half_gram = jax.ShapeDtypeStruct((7 * SIZE // 4, LANES), F32)
    gram = pltpu.VMEM((5 * SIZE // 2, LANES), F32)
    factor = pltpu.VMEM((3 * SIZE, LANES), F32)

    turned = vectors.T
    twin, at, ends = call(
        functools.partial(load_kernel, own_blocks, orbitals),
        [
            jax.ShapeDtypeStruct(turned.shape, BF16),
            jax.ShapeDtypeStruct(columns.shape[::-1], jnp.int32),
            jax.ShapeDtypeStruct((16, LANES), F32),
        ],
        [SMEM] * 2 + [VMEM] * 3,
        name="load",
    )(lower, upper, turned, columns.T, hamiltonian)
    parts = [
        call(pack_kernel, shapes, [VMEM], name="pack")(x) for x in gather_one(turned, twin)
    ]
    start = parts[0]
    terms = summands(own_blocks, at, hamiltonian, parts, COSTS[0])
    first = [
        call(first_kernel, shape, [VMEM] * (2 + len(x)), name="first_filter")(
            ends, vec, *x
        )
        for shape, vec, x in zip(shapes, start, terms)
    ]
    terms = summands(own_blocks, at, hamiltonian, list(zip(*(gather_one(x, x) for x in first))), COSTS[1])
    operands = [x for each in zip(start, first, terms) for x in (each[0], each[1], *each[2])]
    wide, thin, keep, send = call(
        functools.partial(second_kernel, rows_all),
        [*shapes, half_gram, half_gram],
        [VMEM] * (1 + len(operands)),
        [gram],
        name="second_filter",
    )(ends, *operands)
    keep, other = sum_all(keep, send)
    corner = call(
        corner_kernel, jax.ShapeDtypeStruct((SIZE, SIZE), F32), [VMEM], flops=10**9, name="corner"
    )(keep)
    basis = call(
        last_kernel,
        jax.ShapeDtypeStruct((LANES + SIZE, rows), F32),
        [VMEM] * 5,
        [gram, factor, pltpu.VMEM((LANES + SIZE, rows), F32), pltpu.SemaphoreType.DMA((2,))],
        name="orthonormalize",
        out_specs=pl.BlockSpec(memory_space=pl.ANY),
    )(keep, other, corner, wide, thin)
    return basis.T


def solution(mesh):
    return jax.shard_map(
        per_device,
        mesh=mesh,
        in_specs=(
            P(("groups", "row"), None, "col"),
            P(("groups", "row"), "col"),
            P(("groups", "row", "col"), None),
            P("groups"),
            P("groups"),
        ),
        out_specs=P(("groups", "row", "col"), None),
        check_vma=False,
    )
```

```python
import functools

import jax
import jax.numpy as jnp
from jax import lax
from jax.experimental import pallas as pl
from jax.experimental.pallas import tpu as pltpu
from jax.sharding import PartitionSpec as P

LANES = 128
SIZE = LANES // 2
GIGA = 10**9
COSTS = ((3, 1, 3), (3, 0, 0))
F32 = jnp.float32
BF16 = jnp.bfloat16
VMEM = pl.BlockSpec(memory_space=pltpu.VMEM)
SMEM = pl.BlockSpec(memory_space=pltpu.SMEM)


def call(kernel, out_shape, in_specs, scratch=(), flops=1000, name=None, out_specs=None):
    return pl.pallas_call(
        kernel,
        out_shape=out_shape,
        in_specs=in_specs,
        out_specs=out_specs or jax.tree.map(lambda _: VMEM, out_shape),
        scratch_shapes=list(scratch),
        compiler_params=pltpu.CompilerParams(vmem_limit_bytes=40 * 1024 * 1024),
        cost_estimate=pl.CostEstimate(flops=flops, bytes_accessed=1000, transcendentals=0),
        name=name,
    )


def swap(x, axis, key):
    count = lax.axis_size(axis)
    return lax.ppermute(x, axis, [(i, i ^ key) for i in range(count)])


def gather_one(own, twin):
    shards = {0: own}
    bit = lax.axis_size("row") // 2
    while bit:
        for key in list(shards):
            late = key == 0 and bit == 1
            shards[key | bit] = swap(twin if late else shards[key], "row", bit)
        bit //= 2
    return [shards[key] for key in range(len(shards))]


def pack_kernel(turned_ref, wide_out, thin_out):
    rows = turned_ref.shape[1]
    half = rows // 2
    turned = turned_ref[...].astype(F32)
    wide_out[...] = turned[:LANES].T.astype(BF16)
    thin = jnp.concatenate([turned[LANES:, :half], turned[LANES:, half:]], axis=0)
    thin_out[...] = thin.T.astype(BF16)


def load_kernel(
    own_blocks,
    orbitals,
    lower_ref,
    upper_ref,
    vec_ref,
    ids_ref,
    ham_ref,
    vec_out,
    at_out,
    ends_out,
):
    vec_out[...] = vec_ref[...]
    low = jnp.full((8, LANES), lower_ref[0], F32)
    high = jnp.full((8, LANES), upper_ref[0], F32)
    ends_out[pl.ds(0, 8), :] = (high + low) * 0.5
    ends_out[pl.ds(8, 8), :] = 1.0 / ((high - low) * 0.5)
    at_out[...] = (ids_ref[...] ^ (lax.axis_index("row") * own_blocks)) * orbitals


def product_kernel(keys, n_row, own_blocks, at_vmem, ham_ref, *refs):
    wide, thin = refs[:n_row], refs[n_row : 2 * n_row]
    wide_out, thin_out = refs[2 * n_row : 2 * n_row + len(keys)], refs[2 * n_row + len(keys) : -3]
    source, at_ref, sem = refs[-3:]
    copy = pltpu.make_async_copy(at_vmem, at_ref, sem)
    copy.start()
    orbitals = ham_ref.shape[1]
    rows = own_blocks * orbitals
    half = rows // 2
    me = lax.axis_index("col")
    first = [(key ^ me) * own_blocks for key in keys]
    low_lane = lax.broadcasted_iota(jnp.int32, (orbitals, LANES), 1) < SIZE
    for key in range(n_row):
        base = key * rows
        source[pl.ds(base, rows), pl.ds(0, LANES)] = wide[key][...]
        packed = thin[key][...]
        source[pl.ds(base, half), pl.ds(LANES, LANES)] = packed
        source[pl.ds(base + half, half), pl.ds(LANES, LANES)] = jnp.concatenate(
            [packed[:, SIZE:], packed[:, :SIZE]], axis=1
        )

    copy.wait()

    def term(i, block):
        picked = [
            source[pl.ds(pl.multiple_of(at_ref[slot, first[i] + block], orbitals), orbitals), :]
            for slot in range(at_ref.shape[0])
        ]
        return jnp.dot(
            ham_ref[first[i] + block],
            jnp.concatenate(picked, axis=0),
            preferred_element_type=F32,
        )

    for i in range(len(keys)):
        for block in range(own_blocks // 2):
            upper, lower = term(i, block), term(i, block + own_blocks // 2)
            at = pl.ds(block * orbitals, orbitals)
            wide_out[i][at, :] = upper[:, :LANES].astype(BF16)
            wide_out[i][pl.ds(half + block * orbitals, orbitals), :] = lower[:, :LANES].astype(BF16)
            turned = jnp.concatenate([lower[:, LANES + SIZE :], lower[:, LANES : LANES + SIZE]], axis=1)
            thin_out[i][at, :] = jnp.where(low_lane, upper[:, LANES:], turned).astype(BF16)


def product(keys, own_blocks, at, ham, parts):
    n_row = len(parts)
    orbitals = ham.shape[1]
    flops = 4 * own_blocks * len(keys) * orbitals * ham.shape[2] * LANES
    wide, thin = zip(*parts)
    outs = call(
        functools.partial(product_kernel, keys, n_row, own_blocks),
        [jax.ShapeDtypeStruct(x.shape, BF16) for x in parts[0] for _ in keys],
        [VMEM, VMEM] + [VMEM] * (2 * n_row),
        [
            pltpu.VMEM((own_blocks * n_row * orbitals, 2 * LANES), BF16),
            pltpu.SMEM(at.shape, jnp.int32),
            pltpu.SemaphoreType.DMA,
        ],
        flops=flops,
        name="product",
    )(at, ham, *wide, *thin)
    return list(zip(outs[: len(keys)], outs[len(keys) :]))


def add_kernel(a, b, *refs):
    count = len(refs) // 2
    refs[count][...] = (a[...].astype(F32) + b[...].astype(F32)).astype(BF16)
    for later, out in zip(refs[:count], refs[count + 1 :]):
        out[...] = later[...]


def add(a, b, *later, after=(), flops=1000):
    shapes = [jax.ShapeDtypeStruct(x.shape, BF16) for x in (a, *later)]
    count = len(after)
    kernel = lambda *refs: add_kernel(*refs[count:])
    specs = [VMEM] * (count + 2 + len(later))
    return call(kernel, shapes, specs, flops=flops, name="add")(*after, a, b, *later)


def partial_kernel(a, b, out):
    out[...] = a[...].astype(F32) + b[...].astype(F32)


def partial_sum(a, b, flops):
    shape = jax.ShapeDtypeStruct(a.shape, F32)
    return call(partial_kernel, shape, [VMEM] * 2, flops=flops, name="partial_sum")(a, b)


def summands(own_blocks, at, ham, parts, costs):
    n_col = lax.axis_size("col")
    if n_col != 4:
        terms = product(tuple(range(n_col)), own_blocks, at, ham, parts)
        sent = [[swap(x, "col", key) for x in terms[key]] for key in range(1, n_col)]
        return list(zip(terms[0], *sent))
    ((wide, thin),) = product((3,), own_blocks, at, ham, parts)
    wide, thin = swap(wide, "col", 1), swap(thin, "col", 1)
    across, near, own = product((2, 1, 0), own_blocks, at, ham, parts)
    (wide,) = add(across[0], wide)
    thin, *near = add(across[1], thin, *near, after=[wide], flops=costs[0] * GIGA + 1000)
    near = [swap(x, "col", 1) for x in near]
    across = [swap(x, "col", 2) for x in (wide, thin)]
    sums = [
        partial_sum(a, b, cost * GIGA + 1000) for a, b, cost in zip(own, across, costs[1:])
    ]
    return list(zip(sums, near))


def total_of(refs):
    acc = refs[0][...].astype(F32)
    for ref in refs[1:]:
        acc = acc + ref[...].astype(F32)
    return acc


def first_kernel(ends_ref, start, *refs):
    center, scale = ends_ref[pl.ds(0, 1), :], ends_ref[pl.ds(8, 1), :]
    moved = total_of(refs[:-1]) - center * start[...].astype(F32)
    refs[-1][...] = (moved * scale).astype(BF16)


def cross(a, b):
    return lax.dot_general(a, b, (((0,), (0,)), ((), ())), preferred_element_type=F32)


def second_kernel(rows_all, ends_ref, *refs):
    wide_out, thin_out, keep_out, send_out, gram = refs[-5:]
    count = (len(refs) - 5) // 2
    center, scale = ends_ref[pl.ds(0, 1), :], ends_ref[pl.ds(8, 1), :]
    for out, (start, first, *terms) in (
        (wide_out, refs[:count]),
        (thin_out, refs[count : 2 * count]),
    ):
        moved = total_of(terms) - center * first[...].astype(F32)
        out[...] = (2.0 * moved * scale - start[...].astype(F32)).astype(BF16)
    wide, thin = wide_out[...], thin_out[...]
    half = thin.shape[0]
    inv = 1.0 / rows_all
    aa = cross(wide, wide) * inv
    upper = cross(thin, wide[:half]) * inv
    lower = cross(thin, wide[half:]) * inv
    bb = cross(thin, thin) * inv
    bb = bb[:SIZE, :SIZE] + bb[SIZE:, SIZE:]
    corner = fold(aa[:SIZE, :SIZE])
    gram[pl.ds(0, SIZE // 2), :] = fold(bb)
    gram[pl.ds(SIZE // 2, SIZE), :] = aa[SIZE:]
    gram[pl.ds(3 * SIZE // 2, SIZE), :] = upper[:SIZE] + lower[SIZE:]
    part = gram.shape[0] // 2
    mine = lax.axis_index("row") & 1
    for out, half_at in ((keep_out, mine), (send_out, 1 - mine)):
        out[pl.ds(0, SIZE // 2), :] = corner
        out[pl.ds(SIZE // 2, part), :] = gram[pl.ds(pl.multiple_of(half_at * part, 8), part), :]


def fold(block):
    return jnp.concatenate([block[: SIZE // 2], block[SIZE // 2 :]], axis=1)


def unfold(rows):
    return jnp.concatenate([rows[:, :SIZE], rows[:, SIZE:]], axis=0)


def inverse_factor(block):
    size = block.shape[0]
    tiles = size // 8
    rows = lax.broadcasted_iota(jnp.int32, (8, LANES), 0)
    lanes = lax.broadcasted_iota(jnp.int32, (8, LANES), 1)
    pad = jnp.concatenate([block, jnp.zeros((size, LANES - size), F32)], axis=1)
    a = [
        jnp.where(lanes == rows + (size + 8 * t), 1.0, pad[8 * t : 8 * t + 8]) for t in range(tiles)
    ]
    diag = [jnp.ones((8, LANES), F32) for _ in range(tiles)]
    full = (8, LANES)
    def row(x, at):
        return jnp.broadcast_to(x[at : at + 1, :], full)

    def column(x, at):
        return jnp.broadcast_to(x[:, at : at + 1], full)

    def corner(columns):
        return [[row(columns[q], k) for q in range(k + 1)] for k in range(8)]

    small = corner([column(a[0], k) for k in range(8)])
    for t0 in range(tiles):
        j = 8 * t0
        cols = [[column(a[t], j + k) for t in range(t0, tiles)] for k in range(8)]
        lines = [row(a[t0], k) for k in range(8)]
        ahead = t0 + 1 < tiles
        if ahead:
            later = corner([column(a[t0 + 1], j + 8 + k) for k in range(8)])
        for k in range(8):
            d = small[k][k]
            diag[t0] = jnp.where(rows == k, d, diag[t0])
            r = 1.0 / d
            mult = {q: small[q][k] * r for q in range(k + 1, 8)}
            for q in range(k + 1, 8):
                for p in range(k + 1, q + 1):
                    small[q][p] = small[q][p] - mult[q] * small[p][k]
            if ahead:
                below = [row(cols[k][1], q) for q in range(8)]
                for q in range(8):
                    scaled = below[q] * r
                    for p in range(q + 1):
                        later[q][p] = later[q][p] - scaled * below[p]
            for q in range(k + 1, 8):
                lines[q] = lines[q] - mult[q] * lines[k]
            for i, t in enumerate(range(t0, tiles)):
                x = cols[k][i] * r
                if t == t0:
                    x = jnp.where(rows > k, x, 0.0)
                for q in range(k + 1, 8):
                    cols[q][i] = cols[q][i] - cols[k][i] * mult[q]
                a[t] = a[t] - x * lines[k]
        if ahead:
            small = later
    out = jnp.concatenate([a[t] * lax.rsqrt(diag[t]) for t in range(tiles)], axis=0)
    return out[:, size:]


def corner_kernel(keep_ref, out_ref):
    out_ref[...] = inverse_factor(unfold(keep_ref[pl.ds(0, SIZE // 2), :]))


def last_kernel(
    keep_ref, other_ref, corner_ref, wide_ref, thin_ref, out_ref, gram, factor, result, sems
):
    size = LANES // 2
    part = gram.shape[0] // 2
    mine = lax.axis_index("row") & 1
    for ref, half_at in ((keep_ref, mine), (other_ref, 1 - mine)):
        gram[pl.ds(pl.multiple_of(half_at * part, 8), part), :] = ref[pl.ds(size // 2, part), :]
    dot = functools.partial(
        jnp.dot, precision=lax.Precision.HIGHEST, preferred_element_type=F32
    )

    def dot_t(a, b):
        return lax.dot_general(
            a,
            b,
            (((1,), (1,)), ((), ())),
            precision=lax.Precision.HIGHEST,
            preferred_element_type=F32,
        )

    g22 = unfold(gram[pl.ds(0, size // 2), :])
    strip = gram[pl.ds(size // 2, 2 * size), :]
    x0 = corner_ref[...]
    l_strip = dot_t(strip[:, :size], x0)
    rest = strip[:, size:] - dot_t(l_strip, l_strip[:size])
    x1 = inverse_factor(rest[:size])
    l10, l20 = l_strip[:size], l_strip[size:]
    l21 = dot_t(rest[size:], x1)
    last = g22 - dot_t(l20, l20) - dot_t(l21, l21)
    n10 = -dot(x1, dot(l10, x0))
    zero = jnp.zeros((size, size), F32)
    factor[pl.ds(0, size), :] = jnp.concatenate([x0, zero], axis=1)
    factor[pl.ds(size, size), :] = jnp.concatenate([n10, x1], axis=1)

    def apply(mat, vec):
        high = mat.astype(BF16)
        low = (mat - high.astype(F32)).astype(BF16)
        con = (((1,), (1,)), ((), ()))
        return lax.dot_general(high, vec, con, preferred_element_type=F32) + lax.dot_general(
            low, vec, con, preferred_element_type=F32
        )

    wide, thin = wide_ref[...], thin_ref[...]
    half = thin.shape[0]
    head, foot = pl.ds(0, 2 * size), pl.ds(2 * size, size)
    result[head, :] = apply(factor[head, :], wide)
    early = pltpu.make_async_copy(result.at[head], out_ref.at[head], sems.at[0])
    early.start()
    turned = thin.astype(F32).T
    turned = jnp.concatenate([turned[:size], turned[size:]], axis=1)
    rest = turned - dot(jnp.concatenate([l20, l21], axis=1), result[head, :])
    x2 = inverse_factor(last)
    result[foot, :] = dot(x2, rest)
    late = pltpu.make_async_copy(result.at[foot], out_ref.at[foot], sems.at[1])
    late.start()
    early.wait()
    late.wait()


def sum_all(keep, send):
    acc = keep + swap(send, "row", 1)
    bit = 2
    while bit < lax.axis_size("row"):
        acc = acc + swap(acc, "row", bit)
        bit *= 2
    got = [swap(acc, "col", key) for key in range(1, lax.axis_size("col"))]
    for x in got:
        acc = acc + x
    return acc, swap(acc, "row", 1)


def per_device(hamiltonian, columns, vectors, lower, upper):
    rows = vectors.shape[0]
    orbitals = hamiltonian.shape[1]
    own_blocks = rows // orbitals
    rows_all = rows * lax.axis_size("col") * lax.axis_size("row")
    shapes = [jax.ShapeDtypeStruct((x, LANES), BF16) for x in (rows, rows // 2)]
    half_gram = jax.ShapeDtypeStruct((7 * SIZE // 4, LANES), F32)
    gram = pltpu.VMEM((5 * SIZE // 2, LANES), F32)
    factor = pltpu.VMEM((3 * SIZE, LANES), F32)

    turned = vectors.T
    twin, at, ends = call(
        functools.partial(load_kernel, own_blocks, orbitals),
        [
            jax.ShapeDtypeStruct(turned.shape, BF16),
            jax.ShapeDtypeStruct(columns.shape[::-1], jnp.int32),
            jax.ShapeDtypeStruct((16, LANES), F32),
        ],
        [SMEM] * 2 + [VMEM] * 3,
        name="load",
    )(lower, upper, turned, columns.T, hamiltonian)
    parts = [
        call(pack_kernel, shapes, [VMEM], name="pack")(x) for x in gather_one(turned, twin)
    ]
    start = parts[0]
    terms = summands(own_blocks, at, hamiltonian, parts, COSTS[0])
    first = [
        call(first_kernel, shape, [VMEM] * (2 + len(x)), name="first_filter")(
            ends, vec, *x
        )
        for shape, vec, x in zip(shapes, start, terms)
    ]
    terms = summands(own_blocks, at, hamiltonian, list(zip(*(gather_one(x, x) for x in first))), COSTS[1])
    operands = [x for each in zip(start, first, terms) for x in (each[0], each[1], *each[2])]
    wide, thin, keep, send = call(
        functools.partial(second_kernel, rows_all),
        [*shapes, half_gram, half_gram],
        [VMEM] * (1 + len(operands)),
        [gram],
        name="second_filter",
    )(ends, *operands)
    keep, other = sum_all(keep, send)
    corner = call(
        corner_kernel, jax.ShapeDtypeStruct((SIZE, SIZE), F32), [VMEM], flops=10**9, name="corner"
    )(keep)
    basis = call(
        last_kernel,
        jax.ShapeDtypeStruct((LANES + SIZE, rows), F32),
        [VMEM] * 5,
        [gram, factor, pltpu.VMEM((LANES + SIZE, rows), F32), pltpu.SemaphoreType.DMA((2,))],
        name="orthonormalize",
        out_specs=pl.BlockSpec(memory_space=pl.ANY),
    )(keep, other, corner, wide, thin)
    return basis.T


def solution(mesh):
    return jax.shard_map(
        per_device,
        mesh=mesh,
        in_specs=(
            P(("groups", "row"), None, "col"),
            P(("groups", "row"), "col"),
            P(("groups", "row", "col"), None),
            P("groups"),
            P("groups"),
        ),
        out_specs=P(("groups", "row", "col"), None),
        check_vma=False,
    )
```

```python
import functools

import jax
import jax.numpy as jnp
from jax import lax
from jax.experimental import pallas as pl
from jax.experimental.pallas import tpu as pltpu
from jax.sharding import PartitionSpec as P

LANES = 128
SIZE = LANES // 2
GIGA = 10**9
COSTS = ((3, 1, 3, 0, 1), (3, 0, 0, 1))
F32 = jnp.float32
BF16 = jnp.bfloat16
VMEM = pl.BlockSpec(memory_space=pltpu.VMEM)
SMEM = pl.BlockSpec(memory_space=pltpu.SMEM)


def call(kernel, out_shape, in_specs, scratch=(), flops=1000, name=None, out_specs=None):
    return pl.pallas_call(
        kernel,
        out_shape=out_shape,
        in_specs=in_specs,
        out_specs=out_specs or jax.tree.map(lambda _: VMEM, out_shape),
        scratch_shapes=list(scratch),
        compiler_params=pltpu.CompilerParams(vmem_limit_bytes=40 * 1024 * 1024),
        cost_estimate=pl.CostEstimate(flops=flops, bytes_accessed=1000, transcendentals=0),
        name=name,
    )


def swap(x, axis, key):
    count = lax.axis_size(axis)
    return lax.ppermute(x, axis, [(i, i ^ key) for i in range(count)])


def gather_one(own, twin):
    shards = {0: own}
    bit = lax.axis_size("row") // 2
    while bit:
        for key in list(shards):
            late = key == 0 and bit == 1
            shards[key | bit] = swap(twin if late else shards[key], "row", bit)
        bit //= 2
    return [shards[key] for key in range(len(shards))]


def pack_kernel(turned_ref, wide_out, thin_out):
    rows = turned_ref.shape[1]
    half = rows // 2
    turned = turned_ref[...].astype(F32)
    wide_out[...] = turned[:LANES].T.astype(BF16)
    thin = jnp.concatenate([turned[LANES:, :half], turned[LANES:, half:]], axis=0)
    thin_out[...] = thin.T.astype(BF16)


def load_kernel(
    own_blocks,
    orbitals,
    lower_ref,
    upper_ref,
    vec_ref,
    ids_ref,
    ham_ref,
    vec_out,
    at_out,
    ends_out,
):
    vec_out[...] = vec_ref[...]
    low = jnp.full((8, LANES), lower_ref[0], F32)
    high = jnp.full((8, LANES), upper_ref[0], F32)
    ends_out[pl.ds(0, 8), :] = (high + low) * 0.5
    ends_out[pl.ds(8, 8), :] = 1.0 / ((high - low) * 0.5)
    at_out[...] = (ids_ref[...] ^ (lax.axis_index("row") * own_blocks)) * orbitals


def product_kernel(keys, n_row, own_blocks, at_vmem, ham_ref, *refs):
    wide, thin = refs[:n_row], refs[n_row : 2 * n_row]
    wide_out, thin_out = refs[2 * n_row : 2 * n_row + len(keys)], refs[2 * n_row + len(keys) : -3]
    source, at_ref, sem = refs[-3:]
    copy = pltpu.make_async_copy(at_vmem, at_ref, sem)
    copy.start()
    orbitals = ham_ref.shape[1]
    rows = own_blocks * orbitals
    half = rows // 2
    me = lax.axis_index("col")
    first = [(key ^ me) * own_blocks for key in keys]
    low_lane = lax.broadcasted_iota(jnp.int32, (orbitals, LANES), 1) < SIZE
    for key in range(n_row):
        base = key * rows
        source[pl.ds(base, rows), pl.ds(0, LANES)] = wide[key][...]
        packed = thin[key][...]
        source[pl.ds(base, half), pl.ds(LANES, LANES)] = packed
        source[pl.ds(base + half, half), pl.ds(LANES, LANES)] = jnp.concatenate(
            [packed[:, SIZE:], packed[:, :SIZE]], axis=1
        )

    copy.wait()

    def term(i, block):
        picked = [
            source[pl.ds(pl.multiple_of(at_ref[slot, first[i] + block], orbitals), orbitals), :]
            for slot in range(at_ref.shape[0])
        ]
        return jnp.dot(
            ham_ref[first[i] + block],
            jnp.concatenate(picked, axis=0),
            preferred_element_type=F32,
        )

    for i in range(len(keys)):
        for block in range(own_blocks // 2):
            upper, lower = term(i, block), term(i, block + own_blocks // 2)
            at = pl.ds(block * orbitals, orbitals)
            wide_out[i][at, :] = upper[:, :LANES].astype(BF16)
            wide_out[i][pl.ds(half + block * orbitals, orbitals), :] = lower[:, :LANES].astype(BF16)
            turned = jnp.concatenate([lower[:, LANES + SIZE :], lower[:, LANES : LANES + SIZE]], axis=1)
            thin_out[i][at, :] = jnp.where(low_lane, upper[:, LANES:], turned).astype(BF16)


def product(keys, own_blocks, at, ham, parts):
    n_row = len(parts)
    orbitals = ham.shape[1]
    flops = 4 * own_blocks * len(keys) * orbitals * ham.shape[2] * LANES
    wide, thin = zip(*parts)
    outs = call(
        functools.partial(product_kernel, keys, n_row, own_blocks),
        [jax.ShapeDtypeStruct(x.shape, BF16) for x in parts[0] for _ in keys],
        [VMEM, VMEM] + [VMEM] * (2 * n_row),
        [
            pltpu.VMEM((own_blocks * n_row * orbitals, 2 * LANES), BF16),
            pltpu.SMEM(at.shape, jnp.int32),
            pltpu.SemaphoreType.DMA,
        ],
        flops=flops,
        name="product",
    )(at, ham, *wide, *thin)
    return list(zip(outs[: len(keys)], outs[len(keys) :]))


def add_kernel(a, b, *refs):
    count = len(refs) // 2
    refs[count][...] = (a[...].astype(F32) + b[...].astype(F32)).astype(BF16)
    for later, out in zip(refs[:count], refs[count + 1 :]):
        out[...] = later[...]


def add(a, b, *later, after=(), flops=1000):
    shapes = [jax.ShapeDtypeStruct(x.shape, BF16) for x in (a, *later)]
    count = len(after)
    kernel = lambda *refs: add_kernel(*refs[count:])
    specs = [VMEM] * (count + 2 + len(later))
    return call(kernel, shapes, specs, flops=flops, name="add")(*after, a, b, *later)


def partial_kernel(a, b, out):
    out[...] = a[...].astype(F32) + b[...].astype(F32)


def partial_sum(a, b, flops):
    shape = jax.ShapeDtypeStruct(a.shape, F32)
    return call(partial_kernel, shape, [VMEM] * 2, flops=flops, name="partial_sum")(a, b)


def summands(own_blocks, at, ham, parts, costs):
    n_col = lax.axis_size("col")
    if n_col != 4:
        terms = product(tuple(range(n_col)), own_blocks, at, ham, parts)
        sent = [[swap(x, "col", key) for x in terms[key]] for key in range(1, n_col)]
        return list(zip(terms[0], *sent))
    ((wide, thin),) = product((3,), own_blocks, at, ham, parts)
    wide, thin = swap(wide, "col", 1), swap(thin, "col", 1)
    across, near, own = product((2, 1, 0), own_blocks, at, ham, parts)
    (wide,) = add(across[0], wide)
    held = costs[3:]
    thin, *late = add(
        across[1], thin, *(near[i] for i in held), after=[wide], flops=costs[0] * GIGA + 1000
    )
    near = [late[held.index(i)] if i in held else near[i] for i in range(2)]
    near = [swap(x, "col", 1) for x in near]
    across = [swap(x, "col", 2) for x in (wide, thin)]
    sums = [
        partial_sum(a, b, cost * GIGA + 1000) for a, b, cost in zip(own, across, costs[1:3])
    ]
    return list(zip(sums, near))


def total_of(refs):
    acc = refs[0][...].astype(F32)
    for ref in refs[1:]:
        acc = acc + ref[...].astype(F32)
    return acc


def first_kernel(ends_ref, start, *refs):
    center, scale = ends_ref[pl.ds(0, 1), :], ends_ref[pl.ds(8, 1), :]
    moved = total_of(refs[:-1]) - center * start[...].astype(F32)
    refs[-1][...] = (moved * scale).astype(BF16)


def cross(a, b):
    return lax.dot_general(a, b, (((0,), (0,)), ((), ())), preferred_element_type=F32)


def second_kernel(rows_all, ends_ref, *refs):
    wide_out, thin_out, keep_out, send_out, gram = refs[-5:]
    count = (len(refs) - 5) // 2
    center, scale = ends_ref[pl.ds(0, 1), :], ends_ref[pl.ds(8, 1), :]
    for out, (start, first, *terms) in (
        (wide_out, refs[:count]),
        (thin_out, refs[count : 2 * count]),
    ):
        moved = total_of(terms) - center * first[...].astype(F32)
        out[...] = (2.0 * moved * scale - start[...].astype(F32)).astype(BF16)
    wide, thin = wide_out[...], thin_out[...]
    half = thin.shape[0]
    inv = 1.0 / rows_all
    aa = cross(wide, wide) * inv
    upper = cross(thin, wide[:half]) * inv
    lower = cross(thin, wide[half:]) * inv
    bb = cross(thin, thin) * inv
    bb = bb[:SIZE, :SIZE] + bb[SIZE:, SIZE:]
    corner = fold(aa[:SIZE, :SIZE])
    gram[pl.ds(0, SIZE // 2), :] = fold(bb)
    gram[pl.ds(SIZE // 2, SIZE), :] = aa[SIZE:]
    gram[pl.ds(3 * SIZE // 2, SIZE), :] = upper[:SIZE] + lower[SIZE:]
    part = gram.shape[0] // 2
    mine = lax.axis_index("row") & 1
    for out, half_at in ((keep_out, mine), (send_out, 1 - mine)):
        out[pl.ds(0, SIZE // 2), :] = corner
        out[pl.ds(SIZE // 2, part), :] = gram[pl.ds(pl.multiple_of(half_at * part, 8), part), :]


def fold(block):
    return jnp.concatenate([block[: SIZE // 2], block[SIZE // 2 :]], axis=1)


def unfold(rows):
    return jnp.concatenate([rows[:, :SIZE], rows[:, SIZE:]], axis=0)


def inverse_factor(block):
    size = block.shape[0]
    tiles = size // 8
    rows = lax.broadcasted_iota(jnp.int32, (8, LANES), 0)
    lanes = lax.broadcasted_iota(jnp.int32, (8, LANES), 1)
    pad = jnp.concatenate([block, jnp.zeros((size, LANES - size), F32)], axis=1)
    a = [
        jnp.where(lanes == rows + (size + 8 * t), 1.0, pad[8 * t : 8 * t + 8]) for t in range(tiles)
    ]
    diag = [jnp.ones((8, LANES), F32) for _ in range(tiles)]
    full = (8, LANES)
    def row(x, at):
        return jnp.broadcast_to(x[at : at + 1, :], full)

    def column(x, at):
        return jnp.broadcast_to(x[:, at : at + 1], full)

    def corner(columns):
        return [[row(columns[q], k) for q in range(k + 1)] for k in range(8)]

    small = corner([column(a[0], k) for k in range(8)])
    for t0 in range(tiles):
        j = 8 * t0
        cols = [[column(a[t], j + k) for t in range(t0, tiles)] for k in range(8)]
        lines = [row(a[t0], k) for k in range(8)]
        ahead = t0 + 1 < tiles
        if ahead:
            later = corner([column(a[t0 + 1], j + 8 + k) for k in range(8)])
        for k in range(8):
            d = small[k][k]
            diag[t0] = jnp.where(rows == k, d, diag[t0])
            r = 1.0 / d
            mult = {q: small[q][k] * r for q in range(k + 1, 8)}
            for q in range(k + 1, 8):
                for p in range(k + 1, q + 1):
                    small[q][p] = small[q][p] - mult[q] * small[p][k]
            if ahead:
                below = [row(cols[k][1], q) for q in range(8)]
                for q in range(8):
                    scaled = below[q] * r
                    for p in range(q + 1):
                        later[q][p] = later[q][p] - scaled * below[p]
            for q in range(k + 1, 8):
                lines[q] = lines[q] - mult[q] * lines[k]
            for i, t in enumerate(range(t0, tiles)):
                x = cols[k][i] * r
                if t == t0:
                    x = jnp.where(rows > k, x, 0.0)
                for q in range(k + 1, 8):
                    cols[q][i] = cols[q][i] - cols[k][i] * mult[q]
                a[t] = a[t] - x * lines[k]
        if ahead:
            small = later
    out = jnp.concatenate([a[t] * lax.rsqrt(diag[t]) for t in range(tiles)], axis=0)
    return out[:, size:]


def corner_kernel(keep_ref, out_ref):
    out_ref[...] = inverse_factor(unfold(keep_ref[pl.ds(0, SIZE // 2), :]))


def last_kernel(
    keep_ref, other_ref, corner_ref, wide_ref, thin_ref, out_ref, gram, factor, result, sems
):
    size = LANES // 2
    part = gram.shape[0] // 2
    mine = lax.axis_index("row") & 1
    for ref, half_at in ((keep_ref, mine), (other_ref, 1 - mine)):
        gram[pl.ds(pl.multiple_of(half_at * part, 8), part), :] = ref[pl.ds(size // 2, part), :]
    dot = functools.partial(
        jnp.dot, precision=lax.Precision.HIGHEST, preferred_element_type=F32
    )

    def dot_t(a, b):
        return lax.dot_general(
            a,
            b,
            (((1,), (1,)), ((), ())),
            precision=lax.Precision.HIGHEST,
            preferred_element_type=F32,
        )

    g22 = unfold(gram[pl.ds(0, size // 2), :])
    strip = gram[pl.ds(size // 2, 2 * size), :]
    x0 = corner_ref[...]
    l_strip = dot_t(strip[:, :size], x0)
    rest = strip[:, size:] - dot_t(l_strip, l_strip[:size])
    x1 = inverse_factor(rest[:size])
    l10, l20 = l_strip[:size], l_strip[size:]
    l21 = dot_t(rest[size:], x1)
    last = g22 - dot_t(l20, l20) - dot_t(l21, l21)
    n10 = -dot(x1, dot(l10, x0))
    zero = jnp.zeros((size, size), F32)
    factor[pl.ds(0, size), :] = jnp.concatenate([x0, zero], axis=1)
    factor[pl.ds(size, size), :] = jnp.concatenate([n10, x1], axis=1)

    def apply(mat, vec):
        high = mat.astype(BF16)
        low = (mat - high.astype(F32)).astype(BF16)
        con = (((1,), (1,)), ((), ()))
        return lax.dot_general(high, vec, con, preferred_element_type=F32) + lax.dot_general(
            low, vec, con, preferred_element_type=F32
        )

    wide, thin = wide_ref[...], thin_ref[...]
    half = thin.shape[0]
    head, foot = pl.ds(0, 2 * size), pl.ds(2 * size, size)
    result[head, :] = apply(factor[head, :], wide)
    early = pltpu.make_async_copy(result.at[head], out_ref.at[head], sems.at[0])
    early.start()
    turned = thin.astype(F32).T
    turned = jnp.concatenate([turned[:size], turned[size:]], axis=1)
    rest = turned - dot(jnp.concatenate([l20, l21], axis=1), result[head, :])
    x2 = inverse_factor(last)
    result[foot, :] = dot(x2, rest)
    late = pltpu.make_async_copy(result.at[foot], out_ref.at[foot], sems.at[1])
    late.start()
    early.wait()
    late.wait()


def sum_all(keep, send):
    acc = keep + swap(send, "row", 1)
    bit = 2
    while bit < lax.axis_size("row"):
        acc = acc + swap(acc, "row", bit)
        bit *= 2
    got = [swap(acc, "col", key) for key in range(1, lax.axis_size("col"))]
    for x in got:
        acc = acc + x
    return acc, swap(acc, "row", 1)


def per_device(hamiltonian, columns, vectors, lower, upper):
    rows = vectors.shape[0]
    orbitals = hamiltonian.shape[1]
    own_blocks = rows // orbitals
    rows_all = rows * lax.axis_size("col") * lax.axis_size("row")
    shapes = [jax.ShapeDtypeStruct((x, LANES), BF16) for x in (rows, rows // 2)]
    half_gram = jax.ShapeDtypeStruct((7 * SIZE // 4, LANES), F32)
    gram = pltpu.VMEM((5 * SIZE // 2, LANES), F32)
    factor = pltpu.VMEM((3 * SIZE, LANES), F32)

    turned = vectors.T
    twin, at, ends = call(
        functools.partial(load_kernel, own_blocks, orbitals),
        [
            jax.ShapeDtypeStruct(turned.shape, BF16),
            jax.ShapeDtypeStruct(columns.shape[::-1], jnp.int32),
            jax.ShapeDtypeStruct((16, LANES), F32),
        ],
        [SMEM] * 2 + [VMEM] * 3,
        name="load",
    )(lower, upper, turned, columns.T, hamiltonian)
    parts = [
        call(pack_kernel, shapes, [VMEM], name="pack")(x) for x in gather_one(turned, twin)
    ]
    start = parts[0]
    terms = summands(own_blocks, at, hamiltonian, parts, COSTS[0])
    first = [
        call(first_kernel, shape, [VMEM] * (2 + len(x)), name="first_filter")(
            ends, vec, *x
        )
        for shape, vec, x in zip(shapes, start, terms)
    ]
    terms = summands(own_blocks, at, hamiltonian, list(zip(*(gather_one(x, x) for x in first))), COSTS[1])
    operands = [x for each in zip(start, first, terms) for x in (each[0], each[1], *each[2])]
    wide, thin, keep, send = call(
        functools.partial(second_kernel, rows_all),
        [*shapes, half_gram, half_gram],
        [VMEM] * (1 + len(operands)),
        [gram],
        name="second_filter",
    )(ends, *operands)
    keep, other = sum_all(keep, send)
    corner = call(
        corner_kernel, jax.ShapeDtypeStruct((SIZE, SIZE), F32), [VMEM], flops=10**9, name="corner"
    )(keep)
    basis = call(
        last_kernel,
        jax.ShapeDtypeStruct((LANES + SIZE, rows), F32),
        [VMEM] * 5,
        [gram, factor, pltpu.VMEM((LANES + SIZE, rows), F32), pltpu.SemaphoreType.DMA((2,))],
        name="orthonormalize",
        out_specs=pl.BlockSpec(memory_space=pl.ANY),
    )(keep, other, corner, wide, thin)
    return basis.T


def solution(mesh):
    return jax.shard_map(
        per_device,
        mesh=mesh,
        in_specs=(
            P(("groups", "row"), None, "col"),
            P(("groups", "row"), "col"),
            P(("groups", "row", "col"), None),
            P("groups"),
            P("groups"),
        ),
        out_specs=P(("groups", "row", "col"), None),
        check_vma=False,
    )
```
